128 devices in a mesh: grp: 4 (over z_hi, core), row: 32 (over z_lo, y, x).
Axes of the slice: x: 4, y: 4, z: 4 (z_hi: 2, z_lo: 2; z = z_hi * 2 + z_lo), core: 2. Of those that a mesh axis runs over, the one named last changes fastest.
Arguments:
- pair: bfloat16 [1024, 1024, 128], P('row', 'grp'), may hold values from -6 to 6
- token_mask: int32 [1024], replicated, may hold values 0 or 1
- in_gain: float32 [128], replicated, may hold values from 0.5 to 1.5
- in_bias: float32 [128], replicated, may hold values from -3 to 3
- w_in: bfloat16 [128, 512], replicated, may hold values from -0.5 to 0.5
- w_gate: bfloat16 [128, 128], replicated, may hold values from -0.5 to 0.5
- out_gain: float32 [128], replicated, may hold values from 0.5 to 1.5
- out_bias: float32 [128], replicated, may hold values from -3 to 3
- w_out: bfloat16 [128, 128], replicated, may hold values from -0.5 to 0.5
- d_update: bfloat16 [1024, 1024, 128], P('row', 'grp'), may hold values from -6 to 6
Outputs:
- update: bfloat16 [1024, 1024, 128], P('row', 'grp')
- d_pair: bfloat16 [1024, 1024, 128], P('row', 'grp')
- d_w_in: float32 [128, 512], replicated
- d_w_gate: float32 [128, 128], replicated
- d_w_out: float32 [128, 128], replicated
- d_in_norm: float32 [2, 128], replicated
- d_out_norm: float32 [2, 128], replicated
The draws below stay inside these ranges and needn't reach their ends.
Inputs may be any that keep to these rules, and one draw needn't show every extreme that they name: `token_mask`: 1 marks a real token, 0 a padding token.
All inputs are finite; a program needn't handle non-finite values.
Results may differ from the reference program's by a relative error of at most 0.0068.
Values may be sent and summed in bfloat16 or wider, within the bound.
No kernel may reach another device: no remote copies, remote signals or barrier semaphores. Data moves between devices by JAX's collectives and lax.ppermute only.
A program may use at most 128 MiB of HBM per device.

```python
import jax
import jax.numpy as jnp
from jax import lax

PAIR_CH = 128
HID_CH = 128
NTOK = 1024


def plant(values, rng, low, top_value):
    spot = [jax.random.randint(jax.random.fold_in(rng, axis), (), 0, length) for axis, length in enumerate(values.shape)]
    widest = values.shape.index(max(values.shape))
    neighbour = spot[:widest] + [(spot[widest] + 1) % values.shape[widest]] + spot[widest + 1:]
    return values.at[tuple(spot)].set(low).at[tuple(neighbour)].set(top_value)


def shard_levels(rng, dims, pieces, least, largest):
    def one(dim, parts):
        steps = jax.random.uniform(jax.random.fold_in(jax.random.fold_in(rng, 6), dim), (parts,), jnp.float32, least / len(pieces), largest / len(pieces))
        return jnp.repeat(jnp.exp(steps), dims[dim] // parts).reshape((-1,) + (1,) * (len(dims) - dim - 1))

    factor_of = one(*pieces[0])
    for cut in pieces[1:]:
        factor_of = factor_of * one(*cut)
    return factor_of


def noise(rng, shape, deviation, most, split=(), held_as=jnp.bfloat16):
    factor_of = shard_levels(rng, shape, split, -0.22, 0.18) if split else 1.0
    entries = jax.random.normal(rng, shape, jnp.float32) * deviation * factor_of
    return jnp.minimum(jnp.maximum(entries, -most), most).astype(held_as)


def setup_inputs(seed: int = 0) -> dict:
    arg_keys = jax.random.split(jax.random.key(seed), 11)
    pair = noise(arg_keys[0], (NTOK, NTOK, PAIR_CH), 1.0, 6.0, ((0, 32), (1, 4)))
    token_mask = plant((jax.random.randint(arg_keys[1], (NTOK,), 0, 8) < 7).astype(jnp.int32), jax.random.fold_in(arg_keys[1], 1), 0, 1)
    in_gain = jnp.clip(1.0 + 0.1 * jax.random.normal(arg_keys[2], (PAIR_CH,), jnp.float32), 0.5, 1.5)
    in_bias = noise(arg_keys[3], (PAIR_CH,), 0.5, 3.0, (), jnp.float32)
    w_in = noise(arg_keys[4], (PAIR_CH, 4 * HID_CH), PAIR_CH ** -0.5, 0.5)
    w_gate = noise(arg_keys[5], (PAIR_CH, PAIR_CH), PAIR_CH ** -0.5, 0.5)
    out_gain = jnp.clip(1.0 + 0.1 * jax.random.normal(arg_keys[6], (HID_CH,), jnp.float32), 0.5, 1.5)
    out_bias = noise(arg_keys[7], (HID_CH,), 0.5, 3.0, (), jnp.float32)
    w_out = noise(arg_keys[8], (HID_CH, PAIR_CH), HID_CH ** -0.5, 0.5)
    d_update = noise(arg_keys[9], (NTOK, NTOK, PAIR_CH), 1.0, 6.0, ((0, 32), (1, 4)))
    return {"pair": pair, "token_mask": token_mask, "in_gain": in_gain, "in_bias": in_bias, "w_in": w_in, "w_gate": w_gate, "out_gain": out_gain, "out_bias": out_bias, "w_out": w_out, "d_update": d_update}


EPS = 1e-05

def norm_along(values, axis):
    average = lax.optimization_barrier(jnp.mean(values, axis=axis, keepdims=True))
    centered = values - average
    inv_std = lax.rsqrt(lax.optimization_barrier(jnp.mean(centered * centered, axis=axis, keepdims=True)) + EPS)
    return (centered * inv_std, inv_std)

def norm_back(grad_hat, normed_hat, inv_std, axis):
    return inv_std * (grad_hat - lax.optimization_barrier(jnp.mean(grad_hat, axis=axis, keepdims=True)) - normed_hat * lax.optimization_barrier(jnp.mean(grad_hat * normed_hat, axis=axis, keepdims=True)))

def in_side(pair_block, mask_rows, mask_all, in_gain, in_bias, w_in):
    pair_hat, inv_std = norm_along(pair_block.astype(jnp.float32), -1)
    normed = (pair_hat * in_gain + in_bias).astype(jnp.bfloat16)
    projected = jnp.einsum('rjc,cf->frj', normed.astype(jnp.float32), w_in.astype(jnp.float32))
    projected = projected.reshape(2, 2, HID_CH, pair_block.shape[0], pair_block.shape[1])
    edge_gates = jax.nn.sigmoid(projected[:, 0])
    edge_values = projected[:, 1]
    mask_pair = mask_rows[:, None] * mask_all[None, :]
    edge_pairs = (edge_gates * edge_values * mask_pair).astype(jnp.bfloat16)
    return (pair_hat, inv_std, normed, edge_gates, edge_values, mask_pair, edge_pairs)

def reference(pair, token_mask, in_gain, in_bias, w_in, w_gate, out_gain, out_bias, w_out, d_update):
    mask_all = token_mask.astype(jnp.float32)
    row_block = 32
    block_count = NTOK // row_block
    chan_block = 8
    chan_count = HID_CH // chan_block
    pair_blocks = pair.reshape(block_count, row_block, NTOK, PAIR_CH)
    cot_blocks = d_update.reshape(block_count, row_block, NTOK, PAIR_CH)
    mask_blocks = mask_all.reshape(block_count, row_block)

    def forward_edges(operands):
        pair_block, mask_rows = operands
        return in_side(pair_block, mask_rows, mask_all, in_gain, in_bias, w_in)[-1]
    edge_pairs = lax.map(forward_edges, (pair_blocks, mask_blocks))
    edge_pairs = jnp.transpose(edge_pairs, (1, 2, 0, 3, 4)).reshape(2, chan_count, chan_block, NTOK, NTOK)

    def triangle_fwd(operands):
        left_block, right_block = operands
        return jnp.einsum('cki,ckj->cij', left_block.astype(jnp.float32), right_block.astype(jnp.float32)).astype(jnp.bfloat16)
    triangle = lax.map(triangle_fwd, (edge_pairs[0], edge_pairs[1])).reshape(HID_CH, block_count, row_block, NTOK)
    tri_blocks = jnp.transpose(triangle, (1, 0, 2, 3))

    def out_side(totals, operands):
        tri_block, pair_block, mask_rows, cot_block = operands
        normed = in_side(pair_block, mask_rows, mask_all, in_gain, in_bias, w_in)[2]
        tri_hat, tri_inv = norm_along(tri_block.astype(jnp.float32), 0)
        tri_norm = (tri_hat * out_gain[:, None, None] + out_bias[:, None, None]).astype(jnp.bfloat16)
        out_proj = jnp.einsum('crj,cd->rjd', tri_norm.astype(jnp.float32), w_out.astype(jnp.float32))
        out_gate = jax.nn.sigmoid(jnp.einsum('rjc,cd->rjd', normed.astype(jnp.float32), w_gate.astype(jnp.float32)))
        update_block = (out_gate * out_proj).astype(jnp.bfloat16)
        cotangent = cot_block.astype(jnp.float32)
        d_proj = (cotangent * out_gate).astype(jnp.bfloat16)
        d_gate_pre = (cotangent * out_proj * out_gate * (1.0 - out_gate)).astype(jnp.bfloat16)
        sum_out = jnp.einsum('crj,rjd->cd', tri_norm.astype(jnp.float32), d_proj.astype(jnp.float32))
        sum_gate = jnp.einsum('rjc,rjd->cd', normed.astype(jnp.float32), d_gate_pre.astype(jnp.float32))
        d_tri_norm = jnp.einsum('rjd,cd->crj', d_proj.astype(jnp.float32), w_out.astype(jnp.float32))
        sum_norm = jnp.stack([lax.optimization_barrier(jnp.sum(d_tri_norm * tri_hat, axis=(1, 2))), lax.optimization_barrier(jnp.sum(d_tri_norm, axis=(1, 2)))])
        d_triangle = norm_back(d_tri_norm * out_gain[:, None, None], tri_hat, tri_inv, 0).astype(jnp.bfloat16)
        totals = (totals[0] + sum_out, totals[1] + sum_gate, totals[2] + sum_norm)
        return (totals, (update_block, d_triangle, d_gate_pre))
    start = (jnp.zeros((HID_CH, PAIR_CH), jnp.float32), jnp.zeros((PAIR_CH, PAIR_CH), jnp.float32), jnp.zeros((2, HID_CH), jnp.float32))
    totals, (update_blocks, d_tri_blocks, d_gate_blocks) = lax.scan(out_side, start, (tri_blocks, pair_blocks, mask_blocks, cot_blocks))
    d_triangle = jnp.transpose(d_tri_blocks, (1, 0, 2, 3)).reshape(chan_count, chan_block, NTOK, NTOK)

    def triangle_back(operands):
        left_block, right_block, grad_block = operands
        grad_f = grad_block.astype(jnp.float32)
        d_left = jnp.einsum('ckj,cij->cki', right_block.astype(jnp.float32), grad_f).astype(jnp.bfloat16)
        d_right = jnp.einsum('cki,cij->ckj', left_block.astype(jnp.float32), grad_f).astype(jnp.bfloat16)
        return jnp.stack([d_left, d_right])
    d_edges = lax.map(triangle_back, (edge_pairs[0], edge_pairs[1], d_triangle))
    d_edges = jnp.transpose(d_edges, (1, 0, 2, 3, 4)).reshape(2, HID_CH, block_count, row_block, NTOK)
    d_edge_blocks = jnp.transpose(d_edges, (2, 0, 1, 3, 4))

    def back_in(totals, operands):
        pair_block, mask_rows, d_edge_block, d_gate_pre = operands
        pair_hat, inv_std, normed, edge_gates, edge_values, mask_pair, edge_unused = in_side(pair_block, mask_rows, mask_all, in_gain, in_bias, w_in)
        d_edge_f = d_edge_block.astype(jnp.float32) * mask_pair
        d_gate_in = d_edge_f * edge_values * edge_gates * (1.0 - edge_gates)
        d_value_in = d_edge_f * edge_gates
        d_projected = jnp.stack([d_gate_in, d_value_in], axis=1).reshape(4 * HID_CH, row_block, NTOK).astype(jnp.bfloat16)
        sum_in = jnp.einsum('rjc,frj->cf', normed.astype(jnp.float32), d_projected.astype(jnp.float32))
        d_normed = jnp.einsum('frj,cf->rjc', d_projected.astype(jnp.float32), w_in.astype(jnp.float32))
        d_normed = d_normed + jnp.einsum('rjd,cd->rjc', d_gate_pre.astype(jnp.float32), w_gate.astype(jnp.float32))
        sum_norm = jnp.stack([lax.optimization_barrier(jnp.sum(d_normed * pair_hat, axis=(0, 1))), lax.optimization_barrier(jnp.sum(d_normed, axis=(0, 1)))])
        d_pair_block = norm_back(d_normed * in_gain, pair_hat, inv_std, -1).astype(jnp.bfloat16)
        return ((totals[0] + sum_in, totals[1] + sum_norm), d_pair_block)
    start_in = (jnp.zeros((PAIR_CH, 4 * HID_CH), jnp.float32), jnp.zeros((2, PAIR_CH), jnp.float32))
    totals_in, d_pair_blocks = lax.scan(back_in, start_in, (pair_blocks, mask_blocks, d_edge_blocks, d_gate_blocks))
    scale = 1.0 / NTOK
    update = update_blocks.reshape(NTOK, NTOK, PAIR_CH)
    d_pair = d_pair_blocks.reshape(NTOK, NTOK, PAIR_CH)
    return (update, d_pair, totals_in[0] * scale, totals[1] * scale, totals[0] * scale, totals_in[1] * scale, totals[2] * scale)
```

```python
import functools

import jax
import jax.numpy as jnp
from jax import lax
from jax.experimental import pallas as pl
from jax.experimental.pallas import tpu as pltpu
from jax.sharding import PartitionSpec as P

EPS = 1e-05
AXES = ("grp", "row")
RB = 16
F32 = jnp.float32
BF16 = jnp.bfloat16


def dot(lhs, rhs):
    return jnp.dot(lhs, rhs, preferred_element_type=F32)


def dot_nt(lhs, rhs):
    return lax.dot_general(lhs, rhs, (((1,), (1,)), ((), ())), preferred_element_type=F32)


def sigmoid(x):
    return 0.5 + 0.5 * jnp.tanh(0.5 * x)


def columns(vec_row, width):
    chans = vec_row.shape[1]
    return jnp.broadcast_to(vec_row, (width, chans)).T


def norm0(values):
    average = jnp.mean(values, axis=0, keepdims=True)
    centered = values - average
    inv_std = lax.rsqrt(jnp.mean(centered * centered, axis=0, keepdims=True) + EPS)
    return centered * inv_std, inv_std


def norm0_back(grad_hat, normed_hat, inv_std):
    return inv_std * (
        grad_hat
        - jnp.mean(grad_hat, axis=0, keepdims=True)
        - normed_hat * jnp.mean(grad_hat * normed_hat, axis=0, keepdims=True)
    )


def put_rows(scratch, slot, r, values):
    chans, width = values.shape
    for h in range(width // 128):
        scratch[slot + h, pl.ds(r, chans, stride=RB), :] = values[:, h * 128 : (h + 1) * 128]


def get_rows(scratch, slot, r, chans, width):
    return jnp.concatenate(
        [scratch[slot + h, pl.ds(r, chans, stride=RB), :] for h in range(width // 128)], axis=1
    )


def call(kernel, name, grid, ins, outs, scratch, flops, nbytes, args):
    return pl.pallas_call(
        kernel,
        name=name,
        grid=grid,
        in_specs=ins,
        out_specs=[spec for spec, _ in outs],
        out_shape=[shape for _, shape in outs],
        scratch_shapes=scratch,
        compiler_params=pltpu.CompilerParams(vmem_limit_bytes=60 * 1024 * 1024),
        cost_estimate=pl.CostEstimate(flops=flops, bytes_accessed=nbytes, transcendentals=0),
    )(*args)


def whole(shape):
    return pl.BlockSpec(shape, lambda *_: (0,) * len(shape))


def edges_kernel(pair, mask, gain, bias, w_in, edges, pair_t, scr, w_t, cols):
    chans = pair.shape[2]
    width = pair.shape[1]
    hidden = edges.shape[0]

    @pl.when(pl.program_id(0) == 0)
    def _():
        w_t[...] = w_in[...].T
        cols[0] = columns(gain[...], width)
        cols[1] = columns(bias[...], width)

    def step(r, carry):
        x_t = pair[r].T
        pair_t[r] = x_t
        hat, _ = norm0(x_t.astype(F32))
        normed = (hat * cols[0] + cols[1]).astype(BF16)
        proj = dot(w_t[...], normed)
        m = mask[pl.ds(r, 1), :]
        for side in range(2):
            gate = sigmoid(proj[side * 2 * hidden : (side * 2 + 1) * hidden])
            value = proj[(side * 2 + 1) * hidden : (side * 2 + 2) * hidden]
            put_rows(scr, side * (width // 128), r, gate * value * m)
        return carry

    lax.fori_loop(0, RB, step, 0, unroll=2)
    for side in range(2):
        for h in range(width // 128):
            edges[:, side, :, h * 128 : (h + 1) * 128] = (
                scr[side * (width // 128) + h].reshape(hidden, RB, 128).astype(BF16)
            )


def cotangent_kernel(pair_t, d_update, gain, bias, w_gate, d_proj, wg_t, cols):
    width = pair_t.shape[2]

    @pl.when(pl.program_id(0) == 0)
    def _():
        wg_t[...] = w_gate[...].T
        cols[0] = columns(gain[...], width)
        cols[1] = columns(bias[...], width)

    def step(r, carry):
        hat, _ = norm0(pair_t[r].astype(F32))
        normed = (hat * cols[0] + cols[1]).astype(BF16)
        gate = sigmoid(dot(wg_t[...], normed))
        d_proj[r] = (d_update[r].T.astype(F32) * gate).astype(BF16)
        return carry

    lax.fori_loop(0, RB, step, 0, unroll=2)


def triangle_kernel(left, right, out):
    groups, rows, _, tile_rows, width = right.shape
    depth = rows * tile_rows
    left_t = left[...].reshape(depth, width).T
    for h in range(groups):
        out[h] = dot(left_t, right[h].reshape(depth, width)).astype(BF16)


def d_tri_kernel(tri, d_proj, gain, w_out, d_tri, tri_t, scr_in, scr_out, cols):
    hidden, _, width = tri.shape
    halves = width // 128

    @pl.when(pl.program_id(0) == 0)
    def _():
        cols[...] = columns(gain[...], width)

    for h in range(halves):
        scr_in[h] = tri[:, :, h * 128 : (h + 1) * 128].astype(F32).reshape(hidden * RB, 128)

    def step(r, carry):
        t = get_rows(scr_in, 0, r, hidden, width)
        tri_t[r] = t.astype(BF16)
        hat, inv = norm0(t)
        grad = dot(w_out[...], d_proj[r]) * cols[...]
        put_rows(scr_out, 0, r, norm0_back(grad, hat, inv))
        return carry

    lax.fori_loop(0, RB, step, 0, unroll=2)
    for h in range(halves):
        d_tri[:, :, h * 128 : (h + 1) * 128] = (
            scr_out[h].reshape(hidden, RB, 128).astype(BF16)
        )


def update_kernel(
    tri_t, pair_t, d_update, gain, bias, w_gate, o_gain, o_bias, w_out,
    update, d_gate, sum_gate, sum_out, sum_norm,
    wg_t, wo_t, cols, acc,
):
    hidden, width = tri_t.shape[1:]

    @pl.when(pl.program_id(0) == 0)
    def _():
        wg_t[...] = w_gate[...].T
        wo_t[...] = w_out[...].T
        cols[0] = columns(gain[...], width)
        cols[1] = columns(bias[...], width)
        cols[2] = columns(o_gain[...], width)
        cols[3] = columns(o_bias[...], width)
        acc[...] = jnp.zeros_like(acc)
        sum_gate[...] = jnp.zeros_like(sum_gate)
        sum_out[...] = jnp.zeros_like(sum_out)

    def step(r, carry):
        hat, _ = norm0(pair_t[r].astype(F32))
        normed = (hat * cols[0] + cols[1]).astype(BF16)
        gate = sigmoid(dot(wg_t[...], normed))
        cot = d_update[r].T.astype(F32)
        d_proj = (cot * gate).astype(BF16)
        tri_hat, _ = norm0(tri_t[r].astype(F32))
        tri_norm = (tri_hat * cols[2] + cols[3]).astype(BF16)
        out_proj = dot(wo_t[...], tri_norm)
        update[r] = (gate * out_proj).astype(BF16).T
        d_gate_pre = (cot * out_proj * gate * (1.0 - gate)).astype(BF16)
        d_gate[r] = d_gate_pre
        sum_out[...] += dot_nt(tri_norm, d_proj)
        sum_gate[...] += dot_nt(normed, d_gate_pre)
        d_tri_norm = dot(w_out[...], d_proj)
        acc[0] += d_tri_norm * tri_hat
        acc[1] += d_tri_norm
        return carry

    lax.fori_loop(0, RB, step, 0, unroll=2)

    @pl.when(pl.program_id(0) == pl.num_programs(0) - 1)
    def _():
        lane = lax.broadcasted_iota(jnp.int32, (hidden, 128), 1)
        first = jnp.sum(acc[0], axis=1, keepdims=True)
        second = jnp.sum(acc[1], axis=1, keepdims=True)
        sum_norm[...] = jnp.where(lane == 2, first, jnp.where(lane == 3, second, 0.0))


def d_edges_kernel(edges, d_tri, out):
    groups, rows, _, tile_rows, width = edges.shape
    depth = rows * tile_rows
    for g in range(groups):
        left = jnp.zeros((depth, width), F32)
        right = jnp.zeros((depth, width), F32)
        for h in range(groups):
            left += dot_nt(
                edges[h, :, 1].reshape(depth, width), d_tri[h, g * width : (g + 1) * width, :]
            )
            right += dot(
                edges[h, :, 0].reshape(depth, width), d_tri[g, h * width : (h + 1) * width, :]
            )
        out[g, :, 0] = left.astype(BF16).reshape(rows, tile_rows, width)
        out[g, :, 1] = right.astype(BF16).reshape(rows, tile_rows, width)


def back_kernel(
    d_edges, pair_t, d_gate, mask, gain, bias, w_in, w_gate, sum_gate, sum_out, sum_norm,
    d_pair, sums,
    scr, w_t, w_all, cols, acc, acc_in,
):
    hidden = d_edges.shape[0]
    chans, width = pair_t.shape[1:]
    halves = width // 128

    @pl.when(pl.program_id(0) == 0)
    def _():
        w_t[...] = w_in[...].T
        w_all[:, : 4 * hidden] = w_in[...]
        w_all[:, 4 * hidden :] = w_gate[...]
        cols[0] = columns(gain[...], width)
        cols[1] = columns(bias[...], width)
        acc[...] = jnp.zeros_like(acc)
        acc_in[...] = jnp.zeros_like(acc_in)

    for side in range(2):
        for h in range(halves):
            scr[side * halves + h] = (
                d_edges[:, side, :, h * 128 : (h + 1) * 128].astype(F32).reshape(hidden * RB, 128)
            )

    def step(r, carry):
        hat, inv = norm0(pair_t[r].astype(F32))
        normed = (hat * cols[0] + cols[1]).astype(BF16)
        proj = dot(w_t[...], normed)
        m = mask[pl.ds(r, 1), :]
        parts = []
        for side in range(2):
            gate = sigmoid(proj[side * 2 * hidden : (side * 2 + 1) * hidden])
            value = proj[(side * 2 + 1) * hidden : (side * 2 + 2) * hidden]
            d_value = get_rows(scr, side * halves, r, hidden, width) * m * gate
            parts.append((d_value * value * (1.0 - gate)).astype(BF16))
            parts.append(d_value.astype(BF16))
        d_projected = jnp.concatenate(parts, axis=0)
        acc_in[...] += dot_nt(normed, d_projected)
        d_normed = dot(w_all[...], jnp.concatenate([d_projected, d_gate[r]], axis=0))
        acc[0] += d_normed * hat
        acc[1] += d_normed
        d_pair[r] = norm0_back(d_normed * cols[0], hat, inv).astype(BF16).T
        return carry

    lax.fori_loop(0, RB, step, 0, unroll=2)

    @pl.when(pl.program_id(0) == pl.num_programs(0) - 1)
    def _():
        lane = lax.broadcasted_iota(jnp.int32, (hidden, 128), 1)
        first = jnp.sum(acc[0], axis=1, keepdims=True)
        second = jnp.sum(acc[1], axis=1, keepdims=True)
        norms = jnp.where(lane == 0, first, jnp.where(lane == 1, second, sum_norm[...]))
        for q in range(4):
            sums[pl.ds(q, chans, stride=8), :] = acc_in[:, q * 128 : (q + 1) * 128]
        sums[pl.ds(4, chans, stride=8), :] = sum_gate[...]
        sums[pl.ds(5, chans, stride=8), :] = sum_out[...]
        sums[pl.ds(6, chans, stride=8), :] = norms
        sums[pl.ds(7, chans, stride=8), :] = norms


def total_kernel(scale, arrived, out):
    out[...] = jnp.broadcast_to(
        jnp.sum(arrived[...], axis=0, keepdims=True) * scale, out.shape
    )


def unpack_kernel(sums, d_w_in, d_w_gate, d_w_out, d_in_norm, d_out_norm):
    chans = d_w_in.shape[0]
    for q in range(4):
        d_w_in[:, q * 128 : (q + 1) * 128] = sums[pl.ds(q, chans, stride=8), :]
    d_w_gate[...] = sums[pl.ds(4, chans, stride=8), :]
    d_w_out[...] = sums[pl.ds(5, chans, stride=8), :]
    norms = sums[pl.ds(6, chans, stride=8), :].T
    d_in_norm[...] = norms[0:2]
    d_out_norm[...] = norms[2:4]


def exchange(chunks):
    return lax.all_to_all(chunks, AXES, split_axis=0, concat_axis=0, tiled=True)


def body(pair, token_mask, in_gain, in_bias, w_in, w_gate, out_gain, out_bias, w_out, d_update):
    tile_rows, tile_cols, chans = pair.shape
    hidden = w_out.shape[0]
    groups = lax.axis_size("grp")
    rows = lax.axis_size("row")
    tokens = token_mask.shape[0]
    devices = groups * rows
    steps = tile_rows // RB
    halves = tile_cols // 128
    positions = tile_rows * tile_cols
    sds = jax.ShapeDtypeStruct

    mask_all = token_mask.astype(F32)
    row_mask = lax.dynamic_slice_in_dim(mask_all, lax.axis_index("row") * tile_rows, tile_rows)
    col_mask = lax.dynamic_slice_in_dim(mask_all, lax.axis_index("grp") * tile_cols, tile_cols)
    mask_pair = row_mask[:, None] * col_mask[None, :]
    gain, bias = in_gain[None], in_bias[None]
    o_gain, o_bias = out_gain[None], out_bias[None]

    vec = whole((1, chans))
    square = whole((chans, hidden))
    wide = whole((chans, 4 * hidden))
    rowblock = pl.BlockSpec((RB, tile_cols, chans), lambda s: (s, 0, 0))
    chanblock = pl.BlockSpec((RB, chans, tile_cols), lambda s: (s, 0, 0))
    maskblock = pl.BlockSpec((RB, tile_cols), lambda s: (s, 0))
    edgeblock = pl.BlockSpec((hidden, 2, RB, tile_cols), lambda s: (0, 0, s, 0))
    triblock = pl.BlockSpec((hidden, RB, tile_cols), lambda s: (0, s, 0))
    t_shape = sds((tile_rows, chans, tile_cols), BF16)

    edges, pair_t = call(
        edges_kernel, "edges", (steps,),
        [rowblock, maskblock, vec, vec, wide],
        [(edgeblock, sds((hidden, 2, tile_rows, tile_cols), BF16)), (chanblock, t_shape)],
        [
            pltpu.VMEM((2 * halves, hidden * RB, 128), F32),
            pltpu.VMEM((4 * hidden, chans), BF16),
            pltpu.VMEM((2, chans, tile_cols), F32),
        ],
        2 * positions * chans * 4 * hidden, 16 * positions * chans,
        (pair, mask_pair, gain, bias, w_in),
    )
    chan_edges = exchange(edges)
    (d_proj,) = call(
        cotangent_kernel, "cotangent", (steps,),
        [chanblock, rowblock, vec, vec, square],
        [(chanblock, t_shape)],
        [pltpu.VMEM((chans, hidden), BF16), pltpu.VMEM((2, chans, tile_cols), F32)],
        2 * positions * chans * hidden, 8 * positions * chans,
        (pair_t, d_update, gain, bias, w_gate),
    )
    chan_edges = chan_edges.reshape(groups, rows, 2, tile_rows, tile_cols)
    (triangle,) = call(
        triangle_kernel, "triangle", (groups,),
        [
            pl.BlockSpec((1, rows, 1, tile_rows, tile_cols), lambda g: (g, 0, 0, 0, 0)),
            pl.BlockSpec((groups, rows, 1, tile_rows, tile_cols), lambda g: (0, 0, 1, 0, 0)),
        ],
        [
            (
                pl.BlockSpec((groups, tile_cols, tile_cols), lambda g: (0, g, 0)),
                sds((groups, tokens, tile_cols), BF16),
            )
        ],
        [],
        2 * tokens**3, 6 * tokens**2,
        (chan_edges, chan_edges),
    )
    tri = exchange(triangle.reshape(devices, tile_rows, tile_cols))
    d_tri, tri_t = call(
        d_tri_kernel, "d_tri", (steps,),
        [triblock, chanblock, vec, square],
        [(triblock, sds((hidden, tile_rows, tile_cols), BF16)), (chanblock, t_shape)],
        [
            pltpu.VMEM((halves, hidden * RB, 128), F32),
            pltpu.VMEM((halves, hidden * RB, 128), F32),
            pltpu.VMEM((hidden, tile_cols), F32),
        ],
        2 * positions * chans * hidden, 8 * positions * chans,
        (tri, d_proj, o_gain, w_out),
    )
    chan_d_tri = exchange(d_tri)
    update, d_gate, sum_gate, sum_out, sum_norm = call(
        update_kernel, "update", (steps,),
        [chanblock, chanblock, rowblock, vec, vec, square, vec, vec, square],
        [
            (rowblock, sds((tile_rows, tile_cols, chans), BF16)),
            (chanblock, t_shape),
            (square, sds((chans, chans), F32)),
            (square, sds((hidden, chans), F32)),
            (whole((hidden, 128)), sds((hidden, 128), F32)),
        ],
        [
            pltpu.VMEM((chans, chans), BF16),
            pltpu.VMEM((chans, hidden), BF16),
            pltpu.VMEM((4, chans, tile_cols), F32),
            pltpu.VMEM((2, hidden, tile_cols), F32),
        ],
        10 * positions * chans * hidden, 16 * positions * chans,
        (tri_t, pair_t, d_update, gain, bias, w_gate, o_gain, o_bias, w_out),
    )
    depth_rows = rows // groups
    edge_rows = pl.BlockSpec(
        (groups, depth_rows, 2, tile_rows, tile_cols), lambda s: (0, s, 0, 0, 0)
    )
    (d_chan_edges,) = call(
        d_edges_kernel, "d_edges", (groups,),
        [edge_rows, whole((groups, tokens, tile_cols))],
        [(edge_rows, sds((groups, rows, 2, tile_rows, tile_cols), BF16))],
        [],
        4 * tokens**3, 10 * tokens**2,
        (chan_edges, chan_d_tri.reshape(groups, tokens, tile_cols)),
    )
    d_edges = exchange(d_chan_edges.reshape(devices, 2, tile_rows, tile_cols))
    d_pair, sums = call(
        back_kernel, "back", (steps,),
        [edgeblock, chanblock, chanblock, maskblock, vec, vec, wide, square, square, square,
         whole((hidden, 128))],
        [
            (rowblock, sds((tile_rows, tile_cols, chans), BF16)),
            (whole((chans * 8, 128)), sds((chans * 8, 128), F32)),
        ],
        [
            pltpu.VMEM((2 * halves, hidden * RB, 128), F32),
            pltpu.VMEM((4 * hidden, chans), BF16),
            pltpu.VMEM((chans, 4 * hidden + chans), BF16),
            pltpu.VMEM((2, chans, tile_cols), F32),
            pltpu.VMEM((2, chans, tile_cols), F32),
            pltpu.VMEM((chans, 4 * hidden), F32),
        ],
        26 * positions * chans * hidden, 16 * positions * chans,
        (d_edges, pair_t, d_gate, mask_pair, gain, bias, w_in, w_gate, sum_gate, sum_out, sum_norm),
    )
    part = sds((devices, 8, 128), F32)
    arrived = exchange(sums.reshape(devices, 8, 128))
    (total,) = call(
        functools.partial(total_kernel, 1.0 / tokens), "total", (1,),
        [whole(part.shape)], [(whole(part.shape), part)], [],
        devices * 1024, devices * 8192, (arrived,),
    )
    everywhere = exchange(total).reshape(chans * 8, 128)
    small = [
        (chans, 4 * hidden), (chans, chans), (hidden, chans), (2, chans), (2, hidden),
    ]
    grads = call(
        unpack_kernel, "unpack", (1,),
        [whole((chans * 8, 128))],
        [(whole(shape), sds(shape, F32)) for shape in small],
        [], 1024, devices * 8192, (everywhere,),
    )
    return (update, d_pair, *grads)


def solution(mesh):
    return jax.shard_map(
        body,
        mesh=mesh,
        in_specs=(
            P("row", "grp", None),
            P(),
            P(),
            P(),
            P(),
            P(),
            P(),
            P(),
            P(),
            P("row", "grp", None),
        ),
        out_specs=(P("row", "grp", None), P("row", "grp", None), P(), P(), P(), P(), P()),
        check_vma=False,
    )
```

```python
import functools

import jax
import jax.numpy as jnp
from jax import lax
from jax.experimental import pallas as pl
from jax.experimental.pallas import tpu as pltpu
from jax.sharding import PartitionSpec as P

EPS = 1e-05
AXES = ("grp", "row")
RB = 16
BATCH = 4
VMEM_LIMIT = 28 * 1024 * 1024
F32 = jnp.float32
BF16 = jnp.bfloat16


def dot(lhs, rhs):
    return jnp.dot(lhs, rhs, preferred_element_type=F32)


def dot_nt(lhs, rhs):
    return lax.dot_general(lhs, rhs, (((1,), (1,)), ((), ())), preferred_element_type=F32)


def sigmoid(x):
    return 0.5 + 0.5 * jnp.tanh(0.5 * x)


def columns(vec_row, width):
    chans = vec_row.shape[1]
    return jnp.broadcast_to(vec_row, (width, chans)).T


def norm0(values):
    average = jnp.mean(values, axis=0, keepdims=True)
    centered = values - average
    inv_std = lax.rsqrt(jnp.mean(centered * centered, axis=0, keepdims=True) + EPS)
    return centered * inv_std, inv_std


def norm0_back(grad_hat, normed_hat, inv_std):
    return inv_std * (
        grad_hat
        - jnp.mean(grad_hat, axis=0, keepdims=True)
        - normed_hat * jnp.mean(grad_hat * normed_hat, axis=0, keepdims=True)
    )


def fold(values):
    return sum(values[:, i : i + 128] for i in range(0, values.shape[1], 128))


def swap_rows(values):
    return jnp.swapaxes(values, 0, 1)


def call(kernel, name, grid, ins, outs, scratch, flops, nbytes, args, in_hbm=None):
    if in_hbm is None:
        in_hbm = range(len(args))
    args = [
        pltpu.with_memory_space_constraint(arg, pltpu.HBM) if i in in_hbm else arg
        for i, arg in enumerate(args)
    ]
    return pl.pallas_call(
        kernel,
        name=name,
        grid=grid,
        in_specs=ins,
        out_specs=[spec for spec, _ in outs],
        out_shape=[shape for _, shape in outs],
        scratch_shapes=scratch,
        compiler_params=pltpu.CompilerParams(vmem_limit_bytes=VMEM_LIMIT),
        cost_estimate=pl.CostEstimate(flops=flops, bytes_accessed=nbytes, transcendentals=0),
    )(*args)


def whole(shape):
    return pl.BlockSpec(shape, lambda *_: (0,) * len(shape))


def edges_kernel(
    pair, row_tokens, col_tokens, gain, bias, w_in, edges, pair_t, mask, w_t, cols
):
    width = pair.shape[1]
    hidden = edges.shape[0]
    first_row = (lax.axis_index("row") * pl.num_programs(0) + pl.program_id(0)) * RB
    first_col = lax.axis_index("grp") * (width // 128)
    col_mask = jnp.concatenate(
        [col_tokens[pl.ds(first_col + i, 1), :] for i in range(width // 128)], axis=1
    ).astype(F32)

    @pl.when(pl.program_id(0) == 0)
    def _():
        w_t[...] = w_in[...].T
        cols[0] = columns(gain[...], width)
        cols[1] = columns(bias[...], width)

    sides = [[], []]
    for r in range(RB):
        x_t = pair[r].T
        pair_t[r] = x_t
        hat, _ = norm0(x_t.astype(F32))
        normed = (hat * cols[0] + cols[1]).astype(BF16)
        proj = dot(w_t[...], normed)
        m = col_mask * row_tokens[first_row + r].astype(F32)
        mask[r : r + 1, :] = m
        for side in range(2):
            gate = sigmoid(proj[side * 2 * hidden : (side * 2 + 1) * hidden])
            value = proj[(side * 2 + 1) * hidden : (side * 2 + 2) * hidden]
            sides[side].append((gate * value * m).astype(BF16))
    for side in range(2):
        edges[:, side] = swap_rows(jnp.stack(sides[side]))


def cotangent_kernel(pair_t, d_update, gain, bias, w_gate, d_proj, wg_t, cols):
    width = pair_t.shape[2]

    @pl.when(pl.program_id(0) == 0)
    def _():
        wg_t[...] = w_gate[...].T
        cols[0] = columns(gain[...], width)
        cols[1] = columns(bias[...], width)

    for r in range(RB):
        hat, _ = norm0(pair_t[r].astype(F32))
        normed = (hat * cols[0] + cols[1]).astype(BF16)
        gate = sigmoid(dot(wg_t[...], normed))
        d_proj[r] = (d_update[r].T.astype(F32) * gate).astype(BF16)


def triangle_kernel(left, right, out):
    groups, rows, _, tile_rows, width = right.shape
    depth = rows * tile_rows
    left_t = left[...].reshape(depth, width).T
    for h in range(groups):
        out[h] = dot(left_t, right[h].reshape(depth, width)).astype(BF16)


def d_tri_kernel(tri, d_proj, gain, w_out, d_tri, tri_t, cols):
    width = tri.shape[2]

    @pl.when(pl.program_id(0) == 0)
    def _():
        cols[...] = columns(gain[...], width)

    arrived = swap_rows(tri[...])
    tri_t[...] = arrived
    grads = []
    for r in range(RB):
        hat, inv = norm0(arrived[r].astype(F32))
        grad = dot(w_out[...], d_proj[r]) * cols[...]
        grads.append(norm0_back(grad, hat, inv).astype(BF16))
    d_tri[...] = swap_rows(jnp.stack(grads))


def update_kernel(
    tri_t, pair_t, d_update, gain, bias, w_gate, o_gain, o_bias, w_out,
    update, d_gate, sum_gate, sum_out, sum_norm,
    wg_t, wo_t, cols, acc,
):
    hidden, width = tri_t.shape[1:]

    @pl.when(pl.program_id(0) == 0)
    def _():
        wg_t[...] = w_gate[...].T
        wo_t[...] = w_out[...].T
        cols[0] = columns(gain[...], width)
        cols[1] = columns(bias[...], width)
        cols[2] = columns(o_gain[...], width)
        cols[3] = columns(o_bias[...], width)
        acc[...] = jnp.zeros_like(acc)
        sum_gate[...] = jnp.zeros_like(sum_gate)
        sum_out[...] = jnp.zeros_like(sum_out)

    def step(r, carry):
        hat, _ = norm0(pair_t[r].astype(F32))
        normed = (hat * cols[0] + cols[1]).astype(BF16)
        gate = sigmoid(dot(wg_t[...], normed))
        cot = d_update[r].T.astype(F32)
        d_proj = (cot * gate).astype(BF16)
        tri_hat, _ = norm0(tri_t[r].astype(F32))
        tri_norm = (tri_hat * cols[2] + cols[3]).astype(BF16)
        out_proj = dot(wo_t[...], tri_norm)
        update[r] = (gate * out_proj).astype(BF16).T
        d_gate_pre = (cot * out_proj * gate * (1.0 - gate)).astype(BF16)
        d_gate[r] = d_gate_pre
        sum_out[...] += dot_nt(tri_norm, d_proj)
        sum_gate[...] += dot_nt(normed, d_gate_pre)
        d_tri_norm = dot(w_out[...], d_proj)
        acc[0] += fold(d_tri_norm * tri_hat)
        acc[1] += fold(d_tri_norm)
        return carry

    lax.fori_loop(0, RB, step, 0, unroll=4)

    @pl.when(pl.program_id(0) == pl.num_programs(0) - 1)
    def _():
        lane = lax.broadcasted_iota(jnp.int32, (hidden, 128), 1)
        first = jnp.sum(acc[0], axis=1, keepdims=True)
        second = jnp.sum(acc[1], axis=1, keepdims=True)
        sum_norm[...] = jnp.where(lane == 2, first, jnp.where(lane == 3, second, 0.0))


def d_edges_kernel(edges, d_tri, out):
    groups, rows, _, tile_rows, width = edges.shape
    depth = rows * tile_rows
    for g in range(groups):
        left = jnp.zeros((depth, width), F32)
        right = jnp.zeros((depth, width), F32)
        for h in range(groups):
            left += dot_nt(
                edges[h, :, 1].reshape(depth, width), d_tri[h, g * width : (g + 1) * width, :]
            )
            right += dot(
                edges[h, :, 0].reshape(depth, width), d_tri[g, h * width : (h + 1) * width, :]
            )
        out[g, :, 0] = left.astype(BF16).reshape(rows, tile_rows, width)
        out[g, :, 1] = right.astype(BF16).reshape(rows, tile_rows, width)


def back_kernel(
    d_edges, pair_t, d_gate, mask, gain, bias, w_in, w_gate, sum_gate, sum_out, sum_norm,
    d_pair, sums,
    w_t, w_all, cols, acc, acc_in,
):
    hidden = d_edges.shape[0]
    chans, width = pair_t.shape[1:]

    @pl.when(pl.program_id(0) == 0)
    def _():
        w_t[...] = w_in[...].T
        w_all[:, : 4 * hidden] = w_in[...]
        w_all[:, 4 * hidden :] = w_gate[...]
        cols[0] = columns(gain[...], width)
        cols[1] = columns(bias[...], width)
        acc[...] = jnp.zeros_like(acc)
        acc_in[...] = jnp.zeros_like(acc_in)

    arrived = [swap_rows(d_edges[:, side]) for side in range(2)]
    for first_row in range(0, RB, BATCH):
        left, right = [], []
        for r in range(first_row, first_row + BATCH):
            hat, inv = norm0(pair_t[r].astype(F32))
            normed = (hat * cols[0] + cols[1]).astype(BF16)
            proj = dot(w_t[...], normed)
            m = mask[r : r + 1, :]
            parts = []
            for side in range(2):
                gate = sigmoid(proj[side * 2 * hidden : (side * 2 + 1) * hidden])
                value = proj[(side * 2 + 1) * hidden : (side * 2 + 2) * hidden]
                d_value = arrived[side][r].astype(F32) * m * gate
                parts.append((d_value * value * (1.0 - gate)).astype(BF16))
                parts.append(d_value.astype(BF16))
            d_projected = jnp.concatenate(parts, axis=0)
            left.append(normed)
            right.append(d_projected)
            d_normed = dot(w_all[...], jnp.concatenate([d_projected, d_gate[r]], axis=0))
            acc[0] += fold(d_normed * hat)
            acc[1] += fold(d_normed)
            d_pair[r] = norm0_back(d_normed * cols[0], hat, inv).astype(BF16).T
        acc_in[...] += dot_nt(jnp.concatenate(left, axis=1), jnp.concatenate(right, axis=1))

    @pl.when(pl.program_id(0) == pl.num_programs(0) - 1)
    def _():
        lane = lax.broadcasted_iota(jnp.int32, (hidden, 128), 1)
        first = jnp.sum(acc[0], axis=1, keepdims=True)
        second = jnp.sum(acc[1], axis=1, keepdims=True)
        norms = jnp.where(lane == 0, first, jnp.where(lane == 1, second, sum_norm[...]))
        for q in range(4):
            sums[pl.ds(q, chans, stride=8), :] = acc_in[:, q * 128 : (q + 1) * 128]
        sums[pl.ds(4, chans, stride=8), :] = sum_gate[...]
        sums[pl.ds(5, chans, stride=8), :] = sum_out[...]
        sums[pl.ds(6, chans, stride=8), :] = norms
        sums[pl.ds(7, chans, stride=8), :] = norms


def total_kernel(scale, arrived, out):
    out[...] = jnp.broadcast_to(
        jnp.sum(arrived[...], axis=0, keepdims=True) * scale, out.shape
    )


def unpack_kernel(sums, d_w_in, d_w_gate, d_w_out, d_in_norm, d_out_norm):
    chans = d_w_in.shape[0]
    for q in range(4):
        d_w_in[:, q * 128 : (q + 1) * 128] = sums[pl.ds(q, chans, stride=8), :]
    d_w_gate[...] = sums[pl.ds(4, chans, stride=8), :]
    d_w_out[...] = sums[pl.ds(5, chans, stride=8), :]
    norms = sums[pl.ds(6, chans, stride=8), :].T
    d_in_norm[...] = norms[0:2]
    d_out_norm[...] = norms[2:4]


def exchange(chunks):
    return lax.all_to_all(chunks, AXES, split_axis=0, concat_axis=0, tiled=True)


def body(pair, token_mask, in_gain, in_bias, w_in, w_gate, out_gain, out_bias, w_out, d_update):
    tile_rows, tile_cols, chans = pair.shape
    hidden = w_out.shape[0]
    groups = lax.axis_size("grp")
    rows = lax.axis_size("row")
    tokens = token_mask.shape[0]
    devices = groups * rows
    steps = tile_rows // RB
    positions = tile_rows * tile_cols
    sds = jax.ShapeDtypeStruct

    gain, bias = in_gain[None], in_bias[None]
    o_gain, o_bias = out_gain[None], out_bias[None]

    vec = whole((1, chans))
    square = whole((chans, hidden))
    wide = whole((chans, 4 * hidden))
    rowblock = pl.BlockSpec((RB, tile_cols, chans), lambda s: (s, 0, 0))
    chanblock = pl.BlockSpec((RB, chans, tile_cols), lambda s: (s, 0, 0))
    maskblock = pl.BlockSpec((RB, tile_cols), lambda s: (s, 0))
    edgeblock = pl.BlockSpec((hidden, 2, RB, tile_cols), lambda s: (0, 0, s, 0))
    triblock = pl.BlockSpec((hidden, RB, tile_cols), lambda s: (0, s, 0))
    t_shape = sds((tile_rows, chans, tile_cols), BF16)

    edges, pair_t, mask_pair = call(
        edges_kernel, "edges", (steps,),
        [
            rowblock, pl.BlockSpec(memory_space=pltpu.SMEM), whole((tokens // 128, 128)),
            vec, vec, wide,
        ],
        [
            (edgeblock, sds((hidden, 2, tile_rows, tile_cols), BF16)),
            (chanblock, t_shape),
            (maskblock, sds((tile_rows, tile_cols), F32)),
        ],
        [
            pltpu.VMEM((4 * hidden, chans), BF16),
            pltpu.VMEM((2, chans, tile_cols), F32),
        ],
        2 * positions * chans * 4 * hidden, 16 * positions * chans,
        (pair, token_mask, token_mask.reshape(tokens // 128, 128), gain, bias, w_in),
        in_hbm=(0, 2, 3, 4, 5),
    )
    chan_edges = exchange(edges)
    (d_proj,) = call(
        cotangent_kernel, "cotangent", (steps,),
        [chanblock, rowblock, vec, vec, square],
        [(chanblock, pltpu.HBM(t_shape.shape, BF16))],
        [pltpu.VMEM((chans, hidden), BF16), pltpu.VMEM((2, chans, tile_cols), F32)],
        2 * positions * chans * hidden, 8 * positions * chans,
        (pair_t, d_update, gain, bias, w_gate),
    )
    chan_edges = chan_edges.reshape(groups, rows, 2, tile_rows, tile_cols)
    (triangle,) = call(
        triangle_kernel, "triangle", (groups,),
        [
            pl.BlockSpec((1, rows, 1, tile_rows, tile_cols), lambda g: (g, 0, 0, 0, 0)),
            pl.BlockSpec((groups, rows, 1, tile_rows, tile_cols), lambda g: (0, 0, 1, 0, 0)),
        ],
        [
            (
                pl.BlockSpec((groups, tile_cols, tile_cols), lambda g: (0, g, 0)),
                sds((groups, tokens, tile_cols), BF16),
            )
        ],
        [],
        2 * tokens**3, 6 * tokens**2,
        (chan_edges, chan_edges),
        in_hbm=(),
    )
    tri = exchange(triangle.reshape(devices, tile_rows, tile_cols))
    d_tri, tri_t = call(
        d_tri_kernel, "d_tri", (steps,),
        [triblock, chanblock, vec, square],
        [
            (triblock, sds((hidden, tile_rows, tile_cols), BF16)),
            (chanblock, pltpu.HBM(t_shape.shape, BF16)),
        ],
        [
            pltpu.VMEM((hidden, tile_cols), F32),
        ],
        2 * positions * chans * hidden, 8 * positions * chans,
        (tri, d_proj, o_gain, w_out),
        in_hbm=(1, 2, 3),
    )
    chan_d_tri = exchange(d_tri)
    update, d_gate, sum_gate, sum_out, sum_norm = call(
        update_kernel, "update", (steps,),
        [chanblock, chanblock, rowblock, vec, vec, square, vec, vec, square],
        [
            (rowblock, sds((tile_rows, tile_cols, chans), BF16)),
            (chanblock, pltpu.HBM(t_shape.shape, BF16)),
            (square, sds((chans, chans), F32)),
            (square, sds((hidden, chans), F32)),
            (whole((hidden, 128)), sds((hidden, 128), F32)),
        ],
        [
            pltpu.VMEM((chans, chans), BF16),
            pltpu.VMEM((chans, hidden), BF16),
            pltpu.VMEM((4, chans, tile_cols), F32),
            pltpu.VMEM((2, hidden, 128), F32),
        ],
        10 * positions * chans * hidden, 16 * positions * chans,
        (tri_t, pair_t, d_update, gain, bias, w_gate, o_gain, o_bias, w_out),
    )
    depth_rows = rows // groups
    edge_rows = pl.BlockSpec(
        (groups, depth_rows, 2, tile_rows, tile_cols), lambda s: (0, s, 0, 0, 0)
    )
    (d_chan_edges,) = call(
        d_edges_kernel, "d_edges", (groups,),
        [edge_rows, whole((groups, tokens, tile_cols))],
        [(edge_rows, pltpu.HBM((groups, rows, 2, tile_rows, tile_cols), BF16))],
        [],
        4 * tokens**3, 10 * tokens**2,
        (chan_edges, chan_d_tri.reshape(groups, tokens, tile_cols)),
        in_hbm=(),
    )
    d_edges = exchange(d_chan_edges.reshape(devices, 2, tile_rows, tile_cols))
    d_pair, sums = call(
        back_kernel, "back", (steps,),
        [edgeblock, chanblock, chanblock, maskblock, vec, vec, wide, square, square, square,
         whole((hidden, 128))],
        [
            (rowblock, sds((tile_rows, tile_cols, chans), BF16)),
            (whole((chans * 8, 128)), sds((chans * 8, 128), F32)),
        ],
        [
            pltpu.VMEM((4 * hidden, chans), BF16),
            pltpu.VMEM((chans, 4 * hidden + chans), BF16),
            pltpu.VMEM((2, chans, tile_cols), F32),
            pltpu.VMEM((2, chans, 128), F32),
            pltpu.VMEM((chans, 4 * hidden), F32),
        ],
        26 * positions * chans * hidden, 16 * positions * chans,
        (d_edges, pair_t, d_gate, mask_pair, gain, bias, w_in, w_gate, sum_gate, sum_out, sum_norm),
        in_hbm=(0, 1, 2, 4, 5, 6, 7),
    )
    part = sds((devices, 8, 128), F32)
    arrived = exchange(sums.reshape(devices, 8, 128))
    (total,) = call(
        functools.partial(total_kernel, 1.0 / tokens), "total", (1,),
        [whole(part.shape)], [(whole(part.shape), part)], [],
        devices * 1024, devices * 8192, (arrived,),
        in_hbm=(),
    )
    everywhere = exchange(total).reshape(chans * 8, 128)
    small = [
        (chans, 4 * hidden), (chans, chans), (hidden, chans), (2, chans), (2, hidden),
    ]
    grads = call(
        unpack_kernel, "unpack", (1,),
        [whole((chans * 8, 128))],
        [(whole(shape), sds(shape, F32)) for shape in small],
        [], 1024, devices * 8192, (everywhere,),
        in_hbm=(),
    )
    return (update, d_pair, *grads)


def solution(mesh):
    return jax.shard_map(
        body,
        mesh=mesh,
        in_specs=(
            P("row", "grp", None),
            P(),
            P(),
            P(),
            P(),
            P(),
            P(),
            P(),
            P(),
            P("row", "grp", None),
        ),
        out_specs=(P("row", "grp", None), P("row", "grp", None), P(), P(), P(), P(), P()),
        check_vma=False,
    )
```

```python
import functools

import jax
import jax.numpy as jnp
from jax import lax
from jax.experimental import pallas as pl
from jax.experimental.pallas import tpu as pltpu
from jax.sharding import PartitionSpec as P

EPS = 1e-05
AXES = ("grp", "row")
RB = 16
BATCH = 1
VMEM_LIMIT = 28 * 1024 * 1024
F32 = jnp.float32
BF16 = jnp.bfloat16


def dot(lhs, rhs):
    return jnp.dot(lhs, rhs, preferred_element_type=F32)


def dot_nt(lhs, rhs):
    return lax.dot_general(lhs, rhs, (((1,), (1,)), ((), ())), preferred_element_type=F32)


def sigmoid(x):
    return 0.5 + 0.5 * jnp.tanh(0.5 * x)


def columns(vec_row, width):
    chans = vec_row.shape[1]
    return jnp.broadcast_to(vec_row, (width, chans)).T


def norm0(values):
    average = jnp.mean(values, axis=0, keepdims=True)
    centered = values - average
    inv_std = lax.rsqrt(jnp.mean(centered * centered, axis=0, keepdims=True) + EPS)
    return centered * inv_std, inv_std


def norm0_back(grad_hat, normed_hat, inv_std):
    return inv_std * (
        grad_hat
        - jnp.mean(grad_hat, axis=0, keepdims=True)
        - normed_hat * jnp.mean(grad_hat * normed_hat, axis=0, keepdims=True)
    )


def fold(values):
    return sum(values[:, i : i + 128] for i in range(0, values.shape[1], 128))


def swap_rows(values):
    return jnp.swapaxes(values, 0, 1)


def call(kernel, name, grid, ins, outs, scratch, flops, nbytes, args, in_hbm=None):
    if in_hbm is None:
        in_hbm = range(len(args))
    args = [
        pltpu.with_memory_space_constraint(arg, pltpu.HBM) if i in in_hbm else arg
        for i, arg in enumerate(args)
    ]
    return pl.pallas_call(
        kernel,
        name=name,
        grid=grid,
        in_specs=ins,
        out_specs=[spec for spec, _ in outs],
        out_shape=[shape for _, shape in outs],
        scratch_shapes=scratch,
        compiler_params=pltpu.CompilerParams(vmem_limit_bytes=VMEM_LIMIT),
        cost_estimate=pl.CostEstimate(flops=flops, bytes_accessed=nbytes, transcendentals=0),
    )(*args)


def whole(shape):
    return pl.BlockSpec(shape, lambda *_: (0,) * len(shape))


def edges_kernel(
    pair, row_tokens, col_tokens, gain, bias, w_in, edges, mask, w_t, cols
):
    width = pair.shape[1]
    hidden = edges.shape[0]
    first_row = (lax.axis_index("row") * pl.num_programs(0) + pl.program_id(0)) * RB
    first_col = lax.axis_index("grp") * (width // 128)
    col_mask = jnp.concatenate(
        [col_tokens[pl.ds(first_col + i, 1), :] for i in range(width // 128)], axis=1
    ).astype(F32)

    @pl.when(pl.program_id(0) == 0)
    def _():
        w_t[...] = w_in[...].T
        cols[0] = columns(gain[...], width)
        cols[1] = columns(bias[...], width)

    sides = [[], []]
    for r in range(RB):
        hat, _ = norm0(pair[r].T.astype(F32))
        normed = (hat * cols[0] + cols[1]).astype(BF16)
        proj = dot(w_t[...], normed)
        m = col_mask * row_tokens[first_row + r].astype(F32)
        mask[r : r + 1, :] = m
        for side in range(2):
            gate = sigmoid(proj[side * 2 * hidden : (side * 2 + 1) * hidden])
            value = proj[(side * 2 + 1) * hidden : (side * 2 + 2) * hidden]
            sides[side].append((gate * value * m).astype(BF16))
    for side in range(2):
        edges[:, side] = swap_rows(jnp.stack(sides[side]))


def cotangent_kernel(pair, d_update, gain, bias, w_gate, d_proj, pair_t, wg_t, cols):
    width = pair_t.shape[2]

    @pl.when(pl.program_id(0) == 0)
    def _():
        wg_t[...] = w_gate[...].T
        cols[0] = columns(gain[...], width)
        cols[1] = columns(bias[...], width)

    for r in range(RB):
        x_t = pair[r].T
        pair_t[r] = x_t
        hat, _ = norm0(x_t.astype(F32))
        normed = (hat * cols[0] + cols[1]).astype(BF16)
        gate = sigmoid(dot(wg_t[...], normed))
        d_proj[r] = (d_update[r].T.astype(F32) * gate).astype(BF16)


def triangle_kernel(left, right, out):
    groups, rows, _, tile_rows, width = right.shape
    depth = rows * tile_rows
    left_t = left[...].reshape(depth, width).T
    for h in range(groups):
        out[h] = dot(left_t, right[h].reshape(depth, width)).astype(BF16)


def d_tri_kernel(tri, d_proj, gain, w_out, d_tri, cols):
    width = tri.shape[2]

    @pl.when(pl.program_id(0) == 0)
    def _():
        cols[...] = columns(gain[...], width)

    arrived = swap_rows(tri[...])
    grads = []
    for r in range(RB):
        hat, inv = norm0(arrived[r].astype(F32))
        grad = dot(w_out[...], d_proj[r]) * cols[...]
        grads.append(norm0_back(grad, hat, inv).astype(BF16))
    d_tri[...] = swap_rows(jnp.stack(grads))


def update_kernel(
    tri, pair_t, d_update, gain, bias, w_gate, o_gain, o_bias, w_out,
    update, d_gate, sum_gate, sum_out, sum_norm,
    wg_t, wo_t, cols, acc, tri_t,
):
    hidden, _, width = tri.shape
    tri_t[...] = swap_rows(tri[...])

    @pl.when(pl.program_id(0) == 0)
    def _():
        wg_t[...] = w_gate[...].T
        wo_t[...] = w_out[...].T
        cols[0] = columns(gain[...], width)
        cols[1] = columns(bias[...], width)
        cols[2] = columns(o_gain[...], width)
        cols[3] = columns(o_bias[...], width)
        acc[...] = jnp.zeros_like(acc)
        sum_gate[...] = jnp.zeros_like(sum_gate)
        sum_out[...] = jnp.zeros_like(sum_out)

    def step(r, carry):
        hat, _ = norm0(pair_t[r].astype(F32))
        normed = (hat * cols[0] + cols[1]).astype(BF16)
        gate = sigmoid(dot(wg_t[...], normed))
        cot = d_update[r].T.astype(F32)
        d_proj = (cot * gate).astype(BF16)
        tri_hat, _ = norm0(tri_t[r].astype(F32))
        tri_norm = (tri_hat * cols[2] + cols[3]).astype(BF16)
        out_proj = dot(wo_t[...], tri_norm)
        update[r] = (gate * out_proj).astype(BF16).T
        d_gate_pre = (cot * out_proj * gate * (1.0 - gate)).astype(BF16)
        d_gate[r] = d_gate_pre
        sum_out[...] += dot_nt(tri_norm, d_proj)
        sum_gate[...] += dot_nt(normed, d_gate_pre)
        d_tri_norm = dot(w_out[...], d_proj)
        acc[0] += fold(d_tri_norm * tri_hat)
        acc[1] += fold(d_tri_norm)
        return carry

    lax.fori_loop(0, RB, step, 0, unroll=4)

    @pl.when(pl.program_id(0) == pl.num_programs(0) - 1)
    def _():
        lane = lax.broadcasted_iota(jnp.int32, (hidden, 128), 1)
        first = jnp.sum(acc[0], axis=1, keepdims=True)
        second = jnp.sum(acc[1], axis=1, keepdims=True)
        sum_norm[...] = jnp.where(lane == 2, first, jnp.where(lane == 3, second, 0.0))


def d_edges_kernel(edges, d_tri, out):
    groups, rows, _, tile_rows, width = edges.shape
    depth = rows * tile_rows
    for g in range(groups):
        left = jnp.zeros((depth, width), F32)
        right = jnp.zeros((depth, width), F32)
        for h in range(groups):
            left += dot_nt(
                edges[h, :, 1].reshape(depth, width), d_tri[h, g * width : (g + 1) * width, :]
            )
            right += dot(
                edges[h, :, 0].reshape(depth, width), d_tri[g, h * width : (h + 1) * width, :]
            )
        out[g, :, 0] = left.astype(BF16).reshape(rows, tile_rows, width)
        out[g, :, 1] = right.astype(BF16).reshape(rows, tile_rows, width)


def factors_kernel(pair_t, mask, gain, bias, w_in, factors, w_t, cols):
    hidden = w_t.shape[0] // 4
    width = pair_t.shape[2]

    @pl.when(pl.program_id(0) == 0)
    def _():
        w_t[...] = w_in[...].T
        cols[0] = columns(gain[...], width)
        cols[1] = columns(bias[...], width)

    for r in range(RB):
        hat, _ = norm0(pair_t[r].astype(F32))
        normed = (hat * cols[0] + cols[1]).astype(BF16)
        proj = dot(w_t[...], normed)
        m = mask[r : r + 1, :]
        for side in range(2):
            first = side * 2 * hidden
            gate = sigmoid(proj[first : first + hidden])
            value = proj[first + hidden : first + 2 * hidden]
            gate_m = gate * m
            factors[r, first : first + hidden] = (gate_m * value * (1.0 - gate)).astype(BF16)
            factors[r, first + hidden : first + 2 * hidden] = gate_m.astype(BF16)


def back_kernel(
    d_edges, pair_t, d_gate, factors, gain, bias, w_in, w_gate, sum_gate, sum_out, sum_norm,
    d_pair, sums,
    w_all, cols, acc, acc_in, rows_f,
):
    hidden = d_edges.shape[0]
    chans, width = pair_t.shape[1:]

    @pl.when(pl.program_id(0) == 0)
    def _():
        w_all[:, : 4 * hidden] = w_in[...]
        w_all[:, 4 * hidden :] = w_gate[...]
        cols[0] = columns(gain[...], width)
        cols[1] = columns(bias[...], width)
        acc[...] = jnp.zeros_like(acc)
        acc_in[...] = jnp.zeros_like(acc_in)

    arrived = [swap_rows(d_edges[:, side]) for side in range(2)]
    for first_row in range(0, RB, BATCH):
        left, right = [], []
        for r in range(first_row, first_row + BATCH):
            hat, inv = norm0(pair_t[r].astype(F32))
            normed = (hat * cols[0] + cols[1]).astype(BF16)
            d_projected = jnp.concatenate(
                [
                    arrived[part // 2][r] * factors[r, part * hidden : (part + 1) * hidden]
                    for part in range(4)
                ],
                axis=0,
            )
            left.append(normed)
            right.append(d_projected)
            d_normed = dot(w_all[...], jnp.concatenate([d_projected, d_gate[r]], axis=0))
            acc[0] += fold(d_normed * hat)
            acc[1] += fold(d_normed)
            d_pair[r] = norm0_back(d_normed * cols[0], hat, inv).astype(BF16).T
        acc_in[...] += dot_nt(jnp.concatenate(left, axis=1), jnp.concatenate(right, axis=1))

    @pl.when(pl.program_id(0) == pl.num_programs(0) - 1)
    def _():
        lane = lax.broadcasted_iota(jnp.int32, (hidden, 128), 1)
        first = jnp.sum(acc[0], axis=1, keepdims=True)
        second = jnp.sum(acc[1], axis=1, keepdims=True)
        norms = jnp.where(lane == 0, first, jnp.where(lane == 1, second, sum_norm[...]))
        for q in range(4):
            rows_f[pl.ds(q, chans, stride=8), :] = acc_in[:, q * 128 : (q + 1) * 128]
        rows_f[pl.ds(4, chans, stride=8), :] = sum_gate[...]
        rows_f[pl.ds(5, chans, stride=8), :] = sum_out[...]
        rounded = norms.astype(BF16).astype(F32)
        rows_f[pl.ds(6, chans, stride=8), :] = rounded
        rows_f[pl.ds(7, chans, stride=8), :] = norms - rounded
        sums[...] = rows_f[...].reshape(sums.shape).astype(BF16)


def total_kernel(scale, arrived, out):
    total = jnp.sum(arrived[...].astype(F32), axis=0) * scale
    row = lax.broadcasted_iota(jnp.int32, total.shape, 0)
    norms = total[6:7] + total[7:8]
    rounded = norms.astype(BF16).astype(F32)
    total = jnp.where(row == 6, rounded, jnp.where(row == 7, norms - rounded, total))
    out[...] = jnp.broadcast_to(total.astype(BF16)[None], out.shape)


def unpack_kernel(sums, d_w_in, d_w_gate, d_w_out, d_in_norm, d_out_norm, rows_f):
    chans = d_w_in.shape[0]
    rows_f[...] = sums[...].astype(F32).reshape(rows_f.shape)
    for q in range(4):
        d_w_in[:, q * 128 : (q + 1) * 128] = rows_f[pl.ds(q, chans, stride=8), :]
    d_w_gate[...] = rows_f[pl.ds(4, chans, stride=8), :]
    d_w_out[...] = rows_f[pl.ds(5, chans, stride=8), :]
    norms = (rows_f[pl.ds(6, chans, stride=8), :] + rows_f[pl.ds(7, chans, stride=8), :]).T
    d_in_norm[...] = norms[0:2]
    d_out_norm[...] = norms[2:4]


def exchange(chunks):
    return lax.all_to_all(chunks, AXES, split_axis=0, concat_axis=0, tiled=True)


def body(pair, token_mask, in_gain, in_bias, w_in, w_gate, out_gain, out_bias, w_out, d_update):
    tile_rows, tile_cols, chans = pair.shape
    hidden = w_out.shape[0]
    groups = lax.axis_size("grp")
    rows = lax.axis_size("row")
    tokens = token_mask.shape[0]
    devices = groups * rows
    steps = tile_rows // RB
    positions = tile_rows * tile_cols
    sds = jax.ShapeDtypeStruct

    gain, bias = in_gain[None], in_bias[None]
    o_gain, o_bias = out_gain[None], out_bias[None]

    vec = whole((1, chans))
    square = whole((chans, hidden))
    wide = whole((chans, 4 * hidden))
    rowblock = pl.BlockSpec((RB, tile_cols, chans), lambda s: (s, 0, 0))
    chanblock = pl.BlockSpec((RB, chans, tile_cols), lambda s: (s, 0, 0))
    maskblock = pl.BlockSpec((RB, tile_cols), lambda s: (s, 0))
    edgeblock = pl.BlockSpec((hidden, 2, RB, tile_cols), lambda s: (0, 0, s, 0))
    triblock = pl.BlockSpec((hidden, RB, tile_cols), lambda s: (0, s, 0))
    factorblock = pl.BlockSpec((RB, 4 * hidden, tile_cols), lambda s: (s, 0, 0))
    t_shape = sds((tile_rows, chans, tile_cols), BF16)

    edges, mask_pair = call(
        edges_kernel, "edges", (steps,),
        [
            rowblock, pl.BlockSpec(memory_space=pltpu.SMEM), whole((tokens // 128, 128)),
            vec, vec, wide,
        ],
        [
            (edgeblock, sds((hidden, 2, tile_rows, tile_cols), BF16)),
            (maskblock, pltpu.HBM((tile_rows, tile_cols), F32)),
        ],
        [
            pltpu.VMEM((4 * hidden, chans), BF16),
            pltpu.VMEM((2, chans, tile_cols), F32),
        ],
        2 * positions * chans * 4 * hidden, 16 * positions * chans,
        (pair, token_mask, token_mask.reshape(tokens // 128, 128), gain, bias, w_in),
        in_hbm=(0, 2, 3, 4, 5),
    )
    chan_edges = exchange(edges)
    d_proj, pair_t = call(
        cotangent_kernel, "cotangent", (steps,),
        [rowblock, rowblock, vec, vec, square],
        [(chanblock, pltpu.HBM(t_shape.shape, BF16))] * 2,
        [pltpu.VMEM((chans, hidden), BF16), pltpu.VMEM((2, chans, tile_cols), F32)],
        2 * positions * chans * hidden, 8 * positions * chans,
        (pair, d_update, gain, bias, w_gate),
    )
    chan_edges = chan_edges.reshape(groups, rows, 2, tile_rows, tile_cols)
    (triangle,) = call(
        triangle_kernel, "triangle", (groups,),
        [
            pl.BlockSpec((1, rows, 1, tile_rows, tile_cols), lambda g: (g, 0, 0, 0, 0)),
            pl.BlockSpec((groups, rows, 1, tile_rows, tile_cols), lambda g: (0, 0, 1, 0, 0)),
        ],
        [
            (
                pl.BlockSpec((groups, tile_cols, tile_cols), lambda g: (0, g, 0)),
                pltpu.HBM((groups, tokens, tile_cols), BF16),
            )
        ],
        [],
        2 * tokens**3, 6 * tokens**2,
        (chan_edges, chan_edges),
        in_hbm=(),
    )
    tri = exchange(triangle.reshape(devices, tile_rows, tile_cols))
    (d_tri,) = call(
        d_tri_kernel, "d_tri", (steps,),
        [triblock, chanblock, vec, square],
        [
            (triblock, sds((hidden, tile_rows, tile_cols), BF16)),
        ],
        [
            pltpu.VMEM((hidden, tile_cols), F32),
        ],
        2 * positions * chans * hidden, 8 * positions * chans,
        (tri, d_proj, o_gain, w_out),
        in_hbm=(1, 2, 3),
    )
    chan_d_tri = exchange(d_tri)
    update, d_gate, sum_gate, sum_out, sum_norm = call(
        update_kernel, "update", (steps,),
        [triblock, chanblock, rowblock, vec, vec, square, vec, vec, square],
        [
            (rowblock, sds((tile_rows, tile_cols, chans), BF16)),
            (chanblock, pltpu.HBM(t_shape.shape, BF16)),
            (square, sds((chans, chans), F32)),
            (square, sds((hidden, chans), F32)),
            (whole((hidden, 128)), sds((hidden, 128), F32)),
        ],
        [
            pltpu.VMEM((chans, chans), BF16),
            pltpu.VMEM((chans, hidden), BF16),
            pltpu.VMEM((4, chans, tile_cols), F32),
            pltpu.VMEM((2, hidden, 128), F32),
            pltpu.VMEM((RB, hidden, tile_cols), BF16),
        ],
        10 * positions * chans * hidden, 16 * positions * chans,
        (tri, pair_t, d_update, gain, bias, w_gate, o_gain, o_bias, w_out),
    )
    depth_rows = rows // groups
    edge_rows = pl.BlockSpec(
        (groups, depth_rows, 2, tile_rows, tile_cols), lambda s: (0, s, 0, 0, 0)
    )
    (d_chan_edges,) = call(
        d_edges_kernel, "d_edges", (groups,),
        [edge_rows, whole((groups, tokens, tile_cols))],
        [(edge_rows, pltpu.HBM((groups, rows, 2, tile_rows, tile_cols), BF16))],
        [],
        4 * tokens**3, 10 * tokens**2,
        (chan_edges, chan_d_tri.reshape(groups, tokens, tile_cols)),
        in_hbm=(),
    )
    d_edges = exchange(d_chan_edges.reshape(devices, 2, tile_rows, tile_cols))
    (factors,) = call(
        factors_kernel, "factors", (steps,),
        [chanblock, maskblock, vec, vec, wide],
        [(factorblock, pltpu.HBM((tile_rows, 4 * hidden, tile_cols), BF16))],
        [pltpu.VMEM((4 * hidden, chans), BF16), pltpu.VMEM((2, chans, tile_cols), F32)],
        2 * positions * chans * 4 * hidden, 10 * positions * chans,
        (pair_t, mask_pair, gain, bias, w_in),
    )
    d_pair, sums = call(
        back_kernel, "back", (steps,),
        [edgeblock, chanblock, chanblock, factorblock, vec, vec, wide, square, square, square,
         whole((hidden, 128))],
        [
            (rowblock, sds((tile_rows, tile_cols, chans), BF16)),
            (whole((chans, 8, 128)), sds((chans, 8, 128), BF16)),
        ],
        [
            pltpu.VMEM((chans, 4 * hidden + chans), BF16),
            pltpu.VMEM((2, chans, tile_cols), F32),
            pltpu.VMEM((2, chans, 128), F32),
            pltpu.VMEM((chans, 4 * hidden), F32),
            pltpu.VMEM((chans * 8, 128), F32),
        ],
        26 * positions * chans * hidden, 16 * positions * chans,
        (d_edges, pair_t, d_gate, factors, gain, bias, w_in, w_gate, sum_gate, sum_out, sum_norm),
        in_hbm=(0, 1, 2, 3, 4, 5, 6, 7),
    )
    part = sds((devices, 8, 128), BF16)
    arrived = exchange(sums)
    (total,) = call(
        functools.partial(total_kernel, 1.0 / tokens), "total", (1,),
        [whole(part.shape)], [(whole(part.shape), part)], [],
        devices * 1024, devices * 8192, (arrived,),
        in_hbm=(),
    )
    everywhere = exchange(total)
    small = [
        (chans, 4 * hidden), (chans, chans), (hidden, chans), (2, chans), (2, hidden),
    ]
    grads = call(
        unpack_kernel, "unpack", (1,),
        [whole((chans, 8, 128))],
        [(whole(shape), sds(shape, F32)) for shape in small],
        [pltpu.VMEM((chans * 8, 128), F32)], 1024, devices * 8192, (everywhere,),
        in_hbm=(),
    )
    return (update, d_pair, *grads)


def solution(mesh):
    return jax.shard_map(
        body,
        mesh=mesh,
        in_specs=(
            P("row", "grp", None),
            P(),
            P(),
            P(),
            P(),
            P(),
            P(),
            P(),
            P(),
            P("row", "grp", None),
        ),
        out_specs=(P("row", "grp", None), P("row", "grp", None), P(), P(), P(), P(), P()),
        check_vma=False,
    )
```

```python
import functools

import jax
import jax.numpy as jnp
from jax import lax
from jax.experimental import pallas as pl
from jax.experimental.pallas import tpu as pltpu
from jax.sharding import PartitionSpec as P

EPS = 1e-05
AXES = ("grp", "row")
RB = 16
BATCH = 1
VMEM_LIMIT = 28 * 1024 * 1024
F32 = jnp.float32
BF16 = jnp.bfloat16


def dot(lhs, rhs):
    return jnp.dot(lhs, rhs, preferred_element_type=F32)


def dot_nt(lhs, rhs):
    return lax.dot_general(lhs, rhs, (((1,), (1,)), ((), ())), preferred_element_type=F32)


def sigmoid(x):
    return 0.5 + 0.5 * jnp.tanh(0.5 * x)


def columns(vec_row, width):
    chans = vec_row.shape[1]
    return jnp.broadcast_to(vec_row, (width, chans)).T


def norm0(values):
    average = jnp.mean(values, axis=0, keepdims=True)
    centered = values - average
    inv_std = lax.rsqrt(jnp.mean(centered * centered, axis=0, keepdims=True) + EPS)
    return centered * inv_std, inv_std


def norm0_back(grad_hat, normed_hat, inv_std):
    return inv_std * (
        grad_hat
        - jnp.mean(grad_hat, axis=0, keepdims=True)
        - normed_hat * jnp.mean(grad_hat * normed_hat, axis=0, keepdims=True)
    )


def fold(values):
    return sum(values[:, i : i + 128] for i in range(0, values.shape[1], 128))


def swap_rows(values):
    return jnp.swapaxes(values, 0, 1)


def call(kernel, name, grid, ins, outs, scratch, flops, nbytes, args, in_hbm=None):
    if in_hbm is None:
        in_hbm = range(len(args))
    args = [
        pltpu.with_memory_space_constraint(arg, pltpu.HBM) if i in in_hbm else arg
        for i, arg in enumerate(args)
    ]
    return pl.pallas_call(
        kernel,
        name=name,
        grid=grid,
        in_specs=ins,
        out_specs=[spec for spec, _ in outs],
        out_shape=[shape for _, shape in outs],
        scratch_shapes=scratch,
        compiler_params=pltpu.CompilerParams(vmem_limit_bytes=VMEM_LIMIT),
        cost_estimate=pl.CostEstimate(flops=flops, bytes_accessed=nbytes, transcendentals=0),
    )(*args)


def whole(shape):
    return pl.BlockSpec(shape, lambda *_: (0,) * len(shape))


def masks(row_tokens, col_tokens, width):
    first_row = (lax.axis_index("row") * pl.num_programs(0) + pl.program_id(0)) * RB
    first_col = lax.axis_index("grp") * (width // 128)
    col_mask = jnp.concatenate(
        [col_tokens[pl.ds(first_col + i, 1), :] for i in range(width // 128)], axis=1
    ).astype(F32)
    return lambda r: col_mask * row_tokens[first_row + r].astype(F32)


def edges_kernel(
    pair, row_tokens, col_tokens, gain, bias, w_in, edges, w_t, cols
):
    width = pair.shape[1]
    hidden = edges.shape[0]
    row_mask = masks(row_tokens, col_tokens, width)

    @pl.when(pl.program_id(0) == 0)
    def _():
        w_t[...] = w_in[...].T
        cols[0] = columns(gain[...], width)
        cols[1] = columns(bias[...], width)

    sides = [[], []]
    for r in range(RB):
        hat, _ = norm0(pair[r].T.astype(F32))
        normed = (hat * cols[0] + cols[1]).astype(BF16)
        proj = dot(w_t[...], normed)
        m = row_mask(r)
        for side in range(2):
            gate = sigmoid(proj[side * 2 * hidden : (side * 2 + 1) * hidden])
            value = proj[(side * 2 + 1) * hidden : (side * 2 + 2) * hidden]
            sides[side].append((gate * value * m).astype(BF16))
    for side in range(2):
        edges[:, side] = swap_rows(jnp.stack(sides[side]))


def cotangent_kernel(pair, d_update, gain, bias, w_gate, d_proj, pair_t, wg_t, cols):
    width = pair_t.shape[2]

    @pl.when(pl.program_id(0) == 0)
    def _():
        wg_t[...] = w_gate[...].T
        cols[0] = columns(gain[...], width)
        cols[1] = columns(bias[...], width)

    for r in range(RB):
        x_t = pair[r].T
        pair_t[r] = x_t
        hat, _ = norm0(x_t.astype(F32))
        normed = (hat * cols[0] + cols[1]).astype(BF16)
        gate = sigmoid(dot(wg_t[...], normed))
        d_proj[r] = (d_update[r].T.astype(F32) * gate).astype(BF16)


def triangle_kernel(left, right, out):
    groups, rows, _, tile_rows, width = right.shape
    depth = rows * tile_rows
    left_t = left[...].reshape(depth, width).T
    for h in range(groups):
        out[h] = dot(left_t, right[h].reshape(depth, width)).astype(BF16)


def d_tri_kernel(tri, d_proj, gain, w_out, d_tri, cols):
    width = tri.shape[2]

    @pl.when(pl.program_id(0) == 0)
    def _():
        cols[...] = columns(gain[...], width)

    arrived = swap_rows(tri[...])
    grads = []
    for r in range(RB):
        hat, inv = norm0(arrived[r].astype(F32))
        grad = dot(w_out[...], d_proj[r]) * cols[...]
        grads.append(norm0_back(grad, hat, inv).astype(BF16))
    d_tri[...] = swap_rows(jnp.stack(grads))


def update_kernel(
    tri, pair_t, d_update, gain, bias, w_gate, o_gain, o_bias, w_out,
    update, d_gate, sum_gate, sum_out, sum_norm,
    wg_t, wo_t, cols, acc, tri_t,
):
    hidden, _, width = tri.shape
    tri_t[...] = swap_rows(tri[...])

    @pl.when(pl.program_id(0) == 0)
    def _():
        wg_t[...] = w_gate[...].T
        wo_t[...] = w_out[...].T
        cols[0] = columns(gain[...], width)
        cols[1] = columns(bias[...], width)
        cols[2] = columns(o_gain[...], width)
        cols[3] = columns(o_bias[...], width)
        acc[...] = jnp.zeros_like(acc)
        sum_gate[...] = jnp.zeros_like(sum_gate)
        sum_out[...] = jnp.zeros_like(sum_out)

    def step(r, carry):
        hat, _ = norm0(pair_t[r].astype(F32))
        normed = (hat * cols[0] + cols[1]).astype(BF16)
        gate = sigmoid(dot(wg_t[...], normed))
        cot = d_update[r].T.astype(F32)
        d_proj = (cot * gate).astype(BF16)
        tri_hat, _ = norm0(tri_t[r].astype(F32))
        tri_norm = (tri_hat * cols[2] + cols[3]).astype(BF16)
        out_proj = dot(wo_t[...], tri_norm)
        update[r] = (gate * out_proj).astype(BF16).T
        d_gate_pre = (cot * out_proj * gate * (1.0 - gate)).astype(BF16)
        d_gate[r] = d_gate_pre
        sum_out[...] += dot_nt(tri_norm, d_proj)
        sum_gate[...] += dot_nt(normed, d_gate_pre)
        d_tri_norm = dot(w_out[...], d_proj)
        acc[0] += fold(d_tri_norm * tri_hat)
        acc[1] += fold(d_tri_norm)
        return carry

    lax.fori_loop(0, RB, step, 0, unroll=4)

    @pl.when(pl.program_id(0) == pl.num_programs(0) - 1)
    def _():
        lane = lax.broadcasted_iota(jnp.int32, (hidden, 128), 1)
        first = jnp.sum(acc[0], axis=1, keepdims=True)
        second = jnp.sum(acc[1], axis=1, keepdims=True)
        sum_norm[...] = jnp.where(lane == 2, first, jnp.where(lane == 3, second, 0.0))


def d_edges_kernel(edges, d_tri, out):
    groups, rows, _, tile_rows, width = edges.shape
    depth = rows * tile_rows
    for g in range(groups):
        left = jnp.zeros((depth, width), F32)
        right = jnp.zeros((depth, width), F32)
        for h in range(groups):
            left += dot_nt(
                edges[h, :, 1].reshape(depth, width), d_tri[h, g * width : (g + 1) * width, :]
            )
            right += dot(
                edges[h, :, 0].reshape(depth, width), d_tri[g, h * width : (h + 1) * width, :]
            )
        out[g, :, 0] = left.astype(BF16).reshape(rows, tile_rows, width)
        out[g, :, 1] = right.astype(BF16).reshape(rows, tile_rows, width)


def factors_kernel(pair_t, row_tokens, col_tokens, gain, bias, w_in, factors, w_t, cols):
    hidden = w_t.shape[0] // 4
    width = pair_t.shape[2]
    row_mask = masks(row_tokens, col_tokens, width)

    @pl.when(pl.program_id(0) == 0)
    def _():
        w_t[...] = w_in[...].T
        cols[0] = columns(gain[...], width)
        cols[1] = columns(bias[...], width)

    for r in range(RB):
        hat, _ = norm0(pair_t[r].astype(F32))
        normed = (hat * cols[0] + cols[1]).astype(BF16)
        proj = dot(w_t[...], normed)
        m = row_mask(r)
        for side in range(2):
            first = side * 2 * hidden
            gate = sigmoid(proj[first : first + hidden])
            value = proj[first + hidden : first + 2 * hidden]
            gate_m = gate * m
            factors[r, first : first + hidden] = (gate_m * value * (1.0 - gate)).astype(BF16)
            factors[r, first + hidden : first + 2 * hidden] = gate_m.astype(BF16)


def back_kernel(
    d_edges, pair_t, d_gate, factors, gain, bias, w_in, w_gate, sum_gate, sum_out, sum_norm,
    d_pair, sums,
    w_all, cols, acc, acc_in, rows_f,
):
    hidden = d_edges.shape[0]
    chans, width = pair_t.shape[1:]

    @pl.when(pl.program_id(0) == 0)
    def _():
        w_all[:, : 4 * hidden] = w_in[...]
        w_all[:, 4 * hidden :] = w_gate[...]
        cols[0] = columns(gain[...], width)
        cols[1] = columns(bias[...], width)
        acc[...] = jnp.zeros_like(acc)
        acc_in[...] = jnp.zeros_like(acc_in)

    arrived = [swap_rows(d_edges[:, side]) for side in range(2)]
    for first_row in range(0, RB, BATCH):
        left, right = [], []
        for r in range(first_row, first_row + BATCH):
            hat, inv = norm0(pair_t[r].astype(F32))
            normed = (hat * cols[0] + cols[1]).astype(BF16)
            d_projected = jnp.concatenate(
                [
                    arrived[part // 2][r] * factors[r, part * hidden : (part + 1) * hidden]
                    for part in range(4)
                ],
                axis=0,
            )
            left.append(normed)
            right.append(d_projected)
            d_normed = dot(w_all[...], jnp.concatenate([d_projected, d_gate[r]], axis=0))
            acc[0] += fold(d_normed * hat)
            acc[1] += fold(d_normed)
            d_pair[r] = norm0_back(d_normed * cols[0], hat, inv).astype(BF16).T
        acc_in[...] += dot_nt(jnp.concatenate(left, axis=1), jnp.concatenate(right, axis=1))

    @pl.when(pl.program_id(0) == pl.num_programs(0) - 1)
    def _():
        lane = lax.broadcasted_iota(jnp.int32, (hidden, 128), 1)
        first = jnp.sum(acc[0], axis=1, keepdims=True)
        second = jnp.sum(acc[1], axis=1, keepdims=True)
        norms = jnp.where(lane == 0, first, jnp.where(lane == 1, second, sum_norm[...]))
        for q in range(4):
            rows_f[pl.ds(q, chans, stride=8), :] = acc_in[:, q * 128 : (q + 1) * 128]
        rows_f[pl.ds(4, chans, stride=8), :] = sum_gate[...]
        rows_f[pl.ds(5, chans, stride=8), :] = sum_out[...]
        rounded = norms.astype(BF16).astype(F32)
        rows_f[pl.ds(6, chans, stride=8), :] = rounded
        rows_f[pl.ds(7, chans, stride=8), :] = norms - rounded
        sums[...] = rows_f[...].reshape(sums.shape).astype(BF16)


def total_kernel(scale, arrived, out):
    total = jnp.sum(arrived[...].astype(F32), axis=0) * scale
    row = lax.broadcasted_iota(jnp.int32, total.shape, 0)
    norms = total[6:7] + total[7:8]
    rounded = norms.astype(BF16).astype(F32)
    total = jnp.where(row == 6, rounded, jnp.where(row == 7, norms - rounded, total))
    out[...] = jnp.broadcast_to(total.astype(BF16)[None], out.shape)


def unpack_kernel(sums, d_w_in, d_w_gate, d_w_out, d_in_norm, d_out_norm, rows_f):
    chans = d_w_in.shape[0]
    rows_f[...] = sums[...].astype(F32).reshape(rows_f.shape)
    for q in range(4):
        d_w_in[:, q * 128 : (q + 1) * 128] = rows_f[pl.ds(q, chans, stride=8), :]
    d_w_gate[...] = rows_f[pl.ds(4, chans, stride=8), :]
    d_w_out[...] = rows_f[pl.ds(5, chans, stride=8), :]
    norms = (rows_f[pl.ds(6, chans, stride=8), :] + rows_f[pl.ds(7, chans, stride=8), :]).T
    d_in_norm[...] = norms[0:2]
    d_out_norm[...] = norms[2:4]


def exchange(chunks):
    return lax.all_to_all(chunks, AXES, split_axis=0, concat_axis=0, tiled=True)


def body(pair, token_mask, in_gain, in_bias, w_in, w_gate, out_gain, out_bias, w_out, d_update):
    tile_rows, tile_cols, chans = pair.shape
    hidden = w_out.shape[0]
    groups = lax.axis_size("grp")
    rows = lax.axis_size("row")
    tokens = token_mask.shape[0]
    devices = groups * rows
    steps = tile_rows // RB
    positions = tile_rows * tile_cols
    sds = jax.ShapeDtypeStruct

    gain, bias = in_gain[None], in_bias[None]
    o_gain, o_bias = out_gain[None], out_bias[None]

    vec = whole((1, chans))
    square = whole((chans, hidden))
    wide = whole((chans, 4 * hidden))
    rowblock = pl.BlockSpec((RB, tile_cols, chans), lambda s: (s, 0, 0))
    chanblock = pl.BlockSpec((RB, chans, tile_cols), lambda s: (s, 0, 0))
    token_lanes = token_mask.reshape(tokens // 128, 128)
    token_specs = [pl.BlockSpec(memory_space=pltpu.SMEM), whole(token_lanes.shape)]
    edgeblock = pl.BlockSpec((hidden, 2, RB, tile_cols), lambda s: (0, 0, s, 0))
    triblock = pl.BlockSpec((hidden, RB, tile_cols), lambda s: (0, s, 0))
    factorblock = pl.BlockSpec((RB, 4 * hidden, tile_cols), lambda s: (s, 0, 0))
    t_shape = sds((tile_rows, chans, tile_cols), BF16)

    (edges,) = call(
        edges_kernel, "edges", (steps,),
        [
            rowblock, *token_specs, vec, vec, wide,
        ],
        [
            (edgeblock, sds((hidden, 2, tile_rows, tile_cols), BF16)),
        ],
        [
            pltpu.VMEM((4 * hidden, chans), BF16),
            pltpu.VMEM((2, chans, tile_cols), F32),
        ],
        2 * positions * chans * 4 * hidden, 16 * positions * chans,
        (pair, token_mask, token_lanes, gain, bias, w_in),
        in_hbm=(0, 2, 3, 4, 5),
    )
    chan_edges = exchange(edges)
    d_proj, pair_t = call(
        cotangent_kernel, "cotangent", (steps,),
        [rowblock, rowblock, vec, vec, square],
        [(chanblock, pltpu.HBM(t_shape.shape, BF16))] * 2,
        [pltpu.VMEM((chans, hidden), BF16), pltpu.VMEM((2, chans, tile_cols), F32)],
        2 * positions * chans * hidden, 8 * positions * chans,
        (pair, d_update, gain, bias, w_gate),
    )
    chan_edges = chan_edges.reshape(groups, rows, 2, tile_rows, tile_cols)
    (triangle,) = call(
        triangle_kernel, "triangle", (groups,),
        [
            pl.BlockSpec((1, rows, 1, tile_rows, tile_cols), lambda g: (g, 0, 0, 0, 0)),
            pl.BlockSpec((groups, rows, 1, tile_rows, tile_cols), lambda g: (0, 0, 1, 0, 0)),
        ],
        [
            (
                pl.BlockSpec((groups, tile_cols, tile_cols), lambda g: (0, g, 0)),
                pltpu.HBM((groups, tokens, tile_cols), BF16),
            )
        ],
        [],
        2 * tokens**3, 6 * tokens**2,
        (chan_edges, chan_edges),
        in_hbm=(),
    )
    tri = exchange(triangle.reshape(devices, tile_rows, tile_cols))
    (d_tri,) = call(
        d_tri_kernel, "d_tri", (steps,),
        [triblock, chanblock, vec, square],
        [
            (triblock, sds((hidden, tile_rows, tile_cols), BF16)),
        ],
        [
            pltpu.VMEM((hidden, tile_cols), F32),
        ],
        2 * positions * chans * hidden, 8 * positions * chans,
        (tri, d_proj, o_gain, w_out),
        in_hbm=(1, 2, 3),
    )
    chan_d_tri = exchange(d_tri)
    update, d_gate, sum_gate, sum_out, sum_norm = call(
        update_kernel, "update", (steps,),
        [triblock, chanblock, rowblock, vec, vec, square, vec, vec, square],
        [
            (rowblock, sds((tile_rows, tile_cols, chans), BF16)),
            (chanblock, pltpu.HBM(t_shape.shape, BF16)),
            (square, sds((chans, chans), F32)),
            (square, sds((hidden, chans), F32)),
            (whole((hidden, 128)), sds((hidden, 128), F32)),
        ],
        [
            pltpu.VMEM((chans, chans), BF16),
            pltpu.VMEM((chans, hidden), BF16),
            pltpu.VMEM((4, chans, tile_cols), F32),
            pltpu.VMEM((2, hidden, 128), F32),
            pltpu.VMEM((RB, hidden, tile_cols), BF16),
        ],
        10 * positions * chans * hidden, 16 * positions * chans,
        (tri, pair_t, d_update, gain, bias, w_gate, o_gain, o_bias, w_out),
    )
    depth_rows = rows // groups
    edge_rows = pl.BlockSpec(
        (groups, depth_rows, 2, tile_rows, tile_cols), lambda s: (0, s, 0, 0, 0)
    )
    (d_chan_edges,) = call(
        d_edges_kernel, "d_edges", (groups,),
        [edge_rows, whole((groups, tokens, tile_cols))],
        [(edge_rows, pltpu.HBM((groups, rows, 2, tile_rows, tile_cols), BF16))],
        [],
        4 * tokens**3, 10 * tokens**2,
        (chan_edges, chan_d_tri.reshape(groups, tokens, tile_cols)),
        in_hbm=(),
    )
    d_edges = exchange(d_chan_edges.reshape(devices, 2, tile_rows, tile_cols))
    (factors,) = call(
        factors_kernel, "factors", (steps,),
        [chanblock, *token_specs, vec, vec, wide],
        [(factorblock, pltpu.HBM((tile_rows, 4 * hidden, tile_cols), BF16))],
        [pltpu.VMEM((4 * hidden, chans), BF16), pltpu.VMEM((2, chans, tile_cols), F32)],
        2 * positions * chans * 4 * hidden, 10 * positions * chans,
        (pair_t, token_mask, token_lanes, gain, bias, w_in),
        in_hbm=(0, 2, 3, 4, 5),
    )
    d_pair, sums = call(
        back_kernel, "back", (steps,),
        [edgeblock, chanblock, chanblock, factorblock, vec, vec, wide, square, square, square,
         whole((hidden, 128))],
        [
            (rowblock, sds((tile_rows, tile_cols, chans), BF16)),
            (whole((chans, 8, 128)), sds((chans, 8, 128), BF16)),
        ],
        [
            pltpu.VMEM((chans, 4 * hidden + chans), BF16),
            pltpu.VMEM((2, chans, tile_cols), F32),
            pltpu.VMEM((2, chans, 128), F32),
            pltpu.VMEM((chans, 4 * hidden), F32),
            pltpu.VMEM((chans * 8, 128), F32),
        ],
        26 * positions * chans * hidden, 16 * positions * chans,
        (d_edges, pair_t, d_gate, factors, gain, bias, w_in, w_gate, sum_gate, sum_out, sum_norm),
        in_hbm=(1, 2, 3, 4, 5, 6, 7),
    )
    part = sds((devices, 8, 128), BF16)
    arrived = exchange(sums)
    (total,) = call(
        functools.partial(total_kernel, 1.0 / tokens), "total", (1,),
        [whole(part.shape)], [(whole(part.shape), part)], [],
        devices * 1024, devices * 8192, (arrived,),
        in_hbm=(),
    )
    everywhere = exchange(total)
    small = [
        (chans, 4 * hidden), (chans, chans), (hidden, chans), (2, chans), (2, hidden),
    ]
    grads = call(
        unpack_kernel, "unpack", (1,),
        [whole((chans, 8, 128))],
        [(whole(shape), sds(shape, F32)) for shape in small],
        [pltpu.VMEM((chans * 8, 128), F32)], 1024, devices * 8192, (everywhere,),
        in_hbm=(),
    )
    return (update, d_pair, *grads)


def solution(mesh):
    return jax.shard_map(
        body,
        mesh=mesh,
        in_specs=(
            P("row", "grp", None),
            P(),
            P(),
            P(),
            P(),
            P(),
            P(),
            P(),
            P(),
            P("row", "grp", None),
        ),
        out_specs=(P("row", "grp", None), P("row", "grp", None), P(), P(), P(), P(), P()),
        check_vma=False,
    )
```

```python
import functools

import jax
import jax.numpy as jnp
from jax import lax
from jax.experimental import pallas as pl
from jax.experimental.pallas import tpu as pltpu
from jax.sharding import PartitionSpec as P

EPS = 1e-05
AXES = ("grp", "row")
RB = 16
BATCH = 1
VMEM_LIMIT = 28 * 1024 * 1024
F32 = jnp.float32
BF16 = jnp.bfloat16


def dot(lhs, rhs):
    return jnp.dot(lhs, rhs, preferred_element_type=F32)


def dot_nt(lhs, rhs):
    return lax.dot_general(lhs, rhs, (((1,), (1,)), ((), ())), preferred_element_type=F32)


def sigmoid(x):
    return 0.5 + 0.5 * jnp.tanh(0.5 * x)


def columns(vec_row, width):
    chans = vec_row.shape[1]
    return jnp.broadcast_to(vec_row, (width, chans)).T


def norm0(values):
    average = jnp.mean(values, axis=0, keepdims=True)
    centered = values - average
    inv_std = lax.rsqrt(jnp.mean(centered * centered, axis=0, keepdims=True) + EPS)
    return centered * inv_std, inv_std


def norm0_back(grad_hat, normed_hat, inv_std):
    return inv_std * (
        grad_hat
        - jnp.mean(grad_hat, axis=0, keepdims=True)
        - normed_hat * jnp.mean(grad_hat * normed_hat, axis=0, keepdims=True)
    )


def fold(values):
    return sum(values[:, i : i + 128] for i in range(0, values.shape[1], 128))


def swap_rows(values):
    return jnp.swapaxes(values, 0, 1)


def call(kernel, name, grid, ins, outs, scratch, flops, nbytes, args, in_hbm=None):
    if in_hbm is None:
        in_hbm = range(len(args))
    args = [
        pltpu.with_memory_space_constraint(arg, pltpu.HBM) if i in in_hbm else arg
        for i, arg in enumerate(args)
    ]
    return pl.pallas_call(
        kernel,
        name=name,
        grid=grid,
        in_specs=ins,
        out_specs=[spec for spec, _ in outs],
        out_shape=[shape for _, shape in outs],
        scratch_shapes=scratch,
        compiler_params=pltpu.CompilerParams(vmem_limit_bytes=VMEM_LIMIT),
        cost_estimate=pl.CostEstimate(flops=flops, bytes_accessed=nbytes, transcendentals=0),
    )(*args)


def whole(shape):
    return pl.BlockSpec(shape, lambda *_: (0,) * len(shape))


def masks(row_tokens, col_tokens, width):
    first_row = (lax.axis_index("row") * pl.num_programs(0) + pl.program_id(0)) * RB
    first_col = lax.axis_index("grp") * (width // 128)
    col_mask = jnp.concatenate(
        [col_tokens[pl.ds(first_col + i, 1), :] for i in range(width // 128)], axis=1
    ).astype(F32)
    return lambda r: col_mask * row_tokens[first_row + r].astype(F32)


def edges_kernel(
    pair, row_tokens, col_tokens, gain, bias, w_in, edges, w_t, cols
):
    width = pair.shape[1]
    hidden = edges.shape[0]
    row_mask = masks(row_tokens, col_tokens, width)

    @pl.when(pl.program_id(0) == 0)
    def _():
        w_t[...] = w_in[...].T
        cols[0] = columns(gain[...], width)
        cols[1] = columns(bias[...], width)

    sides = [[], []]
    for r in range(RB):
        hat, _ = norm0(pair[r].T.astype(F32))
        normed = (hat * cols[0] + cols[1]).astype(BF16)
        proj = dot(w_t[...], normed)
        m = row_mask(r)
        for side in range(2):
            gate = sigmoid(proj[side * 2 * hidden : (side * 2 + 1) * hidden])
            value = proj[(side * 2 + 1) * hidden : (side * 2 + 2) * hidden]
            sides[side].append((gate * value * m).astype(BF16))
    for side in range(2):
        edges[:, side] = swap_rows(jnp.stack(sides[side]))


def cotangent_kernel(
    pair, d_update, gain, bias, w_gate, o_gain, w_out, grads, pair_t, wg_t, cols
):
    width = pair_t.shape[2]

    @pl.when(pl.program_id(0) == 0)
    def _():
        wg_t[...] = w_gate[...].T
        cols[0] = columns(gain[...], width)
        cols[1] = columns(bias[...], width)
        cols[2] = columns(o_gain[...], width)

    for r in range(RB):
        x_t = pair[r].T
        pair_t[r] = x_t
        hat, _ = norm0(x_t.astype(F32))
        normed = (hat * cols[0] + cols[1]).astype(BF16)
        gate = sigmoid(dot(wg_t[...], normed))
        d_proj = (d_update[r].T.astype(F32) * gate).astype(BF16)
        grad = dot(w_out[...], d_proj) * cols[2]
        grads[r] = grad - jnp.mean(grad, axis=0, keepdims=True)


def triangle_kernel(left, right, out):
    groups, rows, _, tile_rows, width = right.shape
    depth = rows * tile_rows
    left_t = left[...].reshape(depth, width).T
    for h in range(groups):
        out[h] = dot(left_t, right[h].reshape(depth, width)).astype(BF16)


def d_tri_kernel(tri, grads, d_tri):
    arrived = swap_rows(tri[...])
    rows = []
    for r in range(RB):
        hat, inv = norm0(arrived[r].astype(F32))
        grad = grads[r]
        along = jnp.mean(grad * hat, axis=0, keepdims=True)
        rows.append((inv * (grad - hat * along)).astype(BF16))
    d_tri[...] = swap_rows(jnp.stack(rows))


def update_kernel(
    tri, pair_t, d_update, gain, bias, w_gate, o_gain, o_bias, w_out,
    update, d_gate, sum_gate, sum_out, sum_norm,
    wg_t, wo_t, cols, acc, tri_t,
):
    hidden, _, width = tri.shape
    tri_t[...] = swap_rows(tri[...])

    @pl.when(pl.program_id(0) == 0)
    def _():
        wg_t[...] = w_gate[...].T
        wo_t[...] = w_out[...].T
        cols[0] = columns(gain[...], width)
        cols[1] = columns(bias[...], width)
        cols[2] = columns(o_gain[...], width)
        cols[3] = columns(o_bias[...], width)
        acc[...] = jnp.zeros_like(acc)
        sum_gate[...] = jnp.zeros_like(sum_gate)
        sum_out[...] = jnp.zeros_like(sum_out)

    def step(r, carry):
        hat, _ = norm0(pair_t[r].astype(F32))
        normed = (hat * cols[0] + cols[1]).astype(BF16)
        gate = sigmoid(dot(wg_t[...], normed))
        cot = d_update[r].T.astype(F32)
        d_proj = (cot * gate).astype(BF16)
        tri_hat, _ = norm0(tri_t[r].astype(F32))
        tri_norm = (tri_hat * cols[2] + cols[3]).astype(BF16)
        out_proj = dot(wo_t[...], tri_norm)
        update[r] = (gate * out_proj).astype(BF16).T
        d_gate_pre = (cot * out_proj * gate * (1.0 - gate)).astype(BF16)
        d_gate[r] = d_gate_pre
        sum_out[...] += dot_nt(tri_norm, d_proj)
        sum_gate[...] += dot_nt(normed, d_gate_pre)
        d_tri_norm = dot(w_out[...], d_proj)
        acc[0] += fold(d_tri_norm * tri_hat)
        acc[1] += fold(d_tri_norm)
        return carry

    lax.fori_loop(0, RB, step, 0, unroll=4)

    @pl.when(pl.program_id(0) == pl.num_programs(0) - 1)
    def _():
        lane = lax.broadcasted_iota(jnp.int32, (hidden, 128), 1)
        first = jnp.sum(acc[0], axis=1, keepdims=True)
        second = jnp.sum(acc[1], axis=1, keepdims=True)
        sum_norm[...] = jnp.where(lane == 2, first, jnp.where(lane == 3, second, 0.0))


def d_edges_kernel(edges, d_tri, out):
    groups, rows, _, tile_rows, width = edges.shape
    depth = rows * tile_rows
    for g in range(groups):
        left = jnp.zeros((depth, width), F32)
        right = jnp.zeros((depth, width), F32)
        for h in range(groups):
            left += dot_nt(
                edges[h, :, 1].reshape(depth, width), d_tri[h, g * width : (g + 1) * width, :]
            )
            right += dot(
                edges[h, :, 0].reshape(depth, width), d_tri[g, h * width : (h + 1) * width, :]
            )
        out[g, :, 0] = left.astype(BF16).reshape(rows, tile_rows, width)
        out[g, :, 1] = right.astype(BF16).reshape(rows, tile_rows, width)


def factors_kernel(pair_t, row_tokens, col_tokens, gain, bias, w_in, factors, w_t, cols):
    hidden = w_t.shape[0] // 4
    width = pair_t.shape[2]
    row_mask = masks(row_tokens, col_tokens, width)

    @pl.when(pl.program_id(0) == 0)
    def _():
        w_t[...] = w_in[...].T
        cols[0] = columns(gain[...], width)
        cols[1] = columns(bias[...], width)

    for r in range(RB):
        hat, _ = norm0(pair_t[r].astype(F32))
        normed = (hat * cols[0] + cols[1]).astype(BF16)
        proj = dot(w_t[...], normed)
        m = row_mask(r)
        for side in range(2):
            first = side * 2 * hidden
            gate = sigmoid(proj[first : first + hidden])
            value = proj[first + hidden : first + 2 * hidden]
            gate_m = gate * m
            factors[r, first : first + hidden] = (gate_m * value * (1.0 - gate)).astype(BF16)
            factors[r, first + hidden : first + 2 * hidden] = gate_m.astype(BF16)


def back_kernel(
    d_edges, pair_t, d_gate, factors, gain, bias, w_in, w_gate, sum_gate, sum_out, sum_norm,
    d_pair, sums,
    w_all, cols, acc, acc_in, rows_f,
):
    hidden = d_edges.shape[0]
    chans, width = pair_t.shape[1:]

    @pl.when(pl.program_id(0) == 0)
    def _():
        w_all[:, : 4 * hidden] = w_in[...]
        w_all[:, 4 * hidden :] = w_gate[...]
        cols[0] = columns(gain[...], width)
        cols[1] = columns(bias[...], width)
        acc[...] = jnp.zeros_like(acc)
        acc_in[...] = jnp.zeros_like(acc_in)

    arrived = [swap_rows(d_edges[:, side]) for side in range(2)]
    for first_row in range(0, RB, BATCH):
        left, right = [], []
        for r in range(first_row, first_row + BATCH):
            hat, inv = norm0(pair_t[r].astype(F32))
            normed = (hat * cols[0] + cols[1]).astype(BF16)
            d_projected = jnp.concatenate(
                [
                    arrived[part // 2][r] * factors[r, part * hidden : (part + 1) * hidden]
                    for part in range(4)
                ],
                axis=0,
            )
            left.append(normed)
            right.append(d_projected)
            d_normed = dot(w_all[...], jnp.concatenate([d_projected, d_gate[r]], axis=0))
            acc[0] += fold(d_normed * hat)
            acc[1] += fold(d_normed)
            d_pair[r] = norm0_back(d_normed * cols[0], hat, inv).astype(BF16).T
        acc_in[...] += dot_nt(jnp.concatenate(left, axis=1), jnp.concatenate(right, axis=1))

    @pl.when(pl.program_id(0) == pl.num_programs(0) - 1)
    def _():
        lane = lax.broadcasted_iota(jnp.int32, (hidden, 128), 1)
        first = jnp.sum(acc[0], axis=1, keepdims=True)
        second = jnp.sum(acc[1], axis=1, keepdims=True)
        norms = jnp.where(lane == 0, first, jnp.where(lane == 1, second, sum_norm[...]))
        for q in range(4):
            rows_f[pl.ds(q, chans, stride=8), :] = acc_in[:, q * 128 : (q + 1) * 128]
        rows_f[pl.ds(4, chans, stride=8), :] = sum_gate[...]
        rows_f[pl.ds(5, chans, stride=8), :] = sum_out[...]
        rounded = norms.astype(BF16).astype(F32)
        rows_f[pl.ds(6, chans, stride=8), :] = rounded
        rows_f[pl.ds(7, chans, stride=8), :] = norms - rounded
        sums[...] = rows_f[...].reshape(sums.shape).astype(BF16)


def total_kernel(scale, arrived, out):
    total = jnp.sum(arrived[...].astype(F32), axis=0) * scale
    row = lax.broadcasted_iota(jnp.int32, total.shape, 0)
    norms = total[6:7] + total[7:8]
    rounded = norms.astype(BF16).astype(F32)
    total = jnp.where(row == 6, rounded, jnp.where(row == 7, norms - rounded, total))
    out[...] = jnp.broadcast_to(total.astype(BF16)[None], out.shape)


def unpack_kernel(sums, d_w_in, d_w_gate, d_w_out, d_in_norm, d_out_norm, rows_f):
    chans = d_w_in.shape[0]
    rows_f[...] = sums[...].astype(F32).reshape(rows_f.shape)
    for q in range(4):
        d_w_in[:, q * 128 : (q + 1) * 128] = rows_f[pl.ds(q, chans, stride=8), :]
    d_w_gate[...] = rows_f[pl.ds(4, chans, stride=8), :]
    d_w_out[...] = rows_f[pl.ds(5, chans, stride=8), :]
    norms = (rows_f[pl.ds(6, chans, stride=8), :] + rows_f[pl.ds(7, chans, stride=8), :]).T
    d_in_norm[...] = norms[0:2]
    d_out_norm[...] = norms[2:4]


def exchange(chunks):
    return lax.all_to_all(chunks, AXES, split_axis=0, concat_axis=0, tiled=True)


def body(pair, token_mask, in_gain, in_bias, w_in, w_gate, out_gain, out_bias, w_out, d_update):
    tile_rows, tile_cols, chans = pair.shape
    hidden = w_out.shape[0]
    groups = lax.axis_size("grp")
    rows = lax.axis_size("row")
    tokens = token_mask.shape[0]
    devices = groups * rows
    steps = tile_rows // RB
    positions = tile_rows * tile_cols
    sds = jax.ShapeDtypeStruct

    gain, bias = in_gain[None], in_bias[None]
    o_gain, o_bias = out_gain[None], out_bias[None]

    vec = whole((1, chans))
    square = whole((chans, hidden))
    wide = whole((chans, 4 * hidden))
    rowblock = pl.BlockSpec((RB, tile_cols, chans), lambda s: (s, 0, 0))
    chanblock = pl.BlockSpec((RB, chans, tile_cols), lambda s: (s, 0, 0))
    token_lanes = token_mask.reshape(tokens // 128, 128)
    token_specs = [pl.BlockSpec(memory_space=pltpu.SMEM), whole(token_lanes.shape)]
    edgeblock = pl.BlockSpec((hidden, 2, RB, tile_cols), lambda s: (0, 0, s, 0))
    triblock = pl.BlockSpec((hidden, RB, tile_cols), lambda s: (0, s, 0))
    factorblock = pl.BlockSpec((RB, 4 * hidden, tile_cols), lambda s: (s, 0, 0))
    t_shape = sds((tile_rows, chans, tile_cols), BF16)

    (edges,) = call(
        edges_kernel, "edges", (steps,),
        [
            rowblock, *token_specs, vec, vec, wide,
        ],
        [
            (edgeblock, sds((hidden, 2, tile_rows, tile_cols), BF16)),
        ],
        [
            pltpu.VMEM((4 * hidden, chans), BF16),
            pltpu.VMEM((2, chans, tile_cols), F32),
        ],
        2 * positions * chans * 4 * hidden, 16 * positions * chans,
        (pair, token_mask, token_lanes, gain, bias, w_in),
        in_hbm=(0, 2, 3, 4, 5),
    )
    chan_edges = exchange(edges)
    grads, pair_t = call(
        cotangent_kernel, "cotangent", (steps,),
        [rowblock, rowblock, vec, vec, square, vec, square],
        [
            (chanblock, pltpu.HBM(t_shape.shape, F32)),
            (chanblock, pltpu.HBM(t_shape.shape, BF16)),
        ],
        [pltpu.VMEM((chans, hidden), BF16), pltpu.VMEM((3, chans, tile_cols), F32)],
        2 * positions * chans * hidden, 8 * positions * chans,
        (pair, d_update, gain, bias, w_gate, o_gain, w_out),
    )
    chan_edges = chan_edges.reshape(groups, rows, 2, tile_rows, tile_cols)
    (triangle,) = call(
        triangle_kernel, "triangle", (groups,),
        [
            pl.BlockSpec((1, rows, 1, tile_rows, tile_cols), lambda g: (g, 0, 0, 0, 0)),
            pl.BlockSpec((groups, rows, 1, tile_rows, tile_cols), lambda g: (0, 0, 1, 0, 0)),
        ],
        [
            (
                pl.BlockSpec((groups, tile_cols, tile_cols), lambda g: (0, g, 0)),
                pltpu.HBM((groups, tokens, tile_cols), BF16),
            )
        ],
        [],
        2 * tokens**3, 6 * tokens**2,
        (chan_edges, chan_edges),
        in_hbm=(),
    )
    tri = exchange(triangle.reshape(devices, tile_rows, tile_cols))
    (d_tri,) = call(
        d_tri_kernel, "d_tri", (steps,),
        [triblock, chanblock],
        [
            (triblock, sds((hidden, tile_rows, tile_cols), BF16)),
        ],
        [],
        2 * positions * chans * hidden, 8 * positions * chans,
        (tri, grads),
        in_hbm=(1,),
    )
    chan_d_tri = exchange(d_tri)
    update, d_gate, sum_gate, sum_out, sum_norm = call(
        update_kernel, "update", (steps,),
        [triblock, chanblock, rowblock, vec, vec, square, vec, vec, square],
        [
            (rowblock, sds((tile_rows, tile_cols, chans), BF16)),
            (chanblock, pltpu.HBM(t_shape.shape, BF16)),
            (square, sds((chans, chans), F32)),
            (square, sds((hidden, chans), F32)),
            (whole((hidden, 128)), sds((hidden, 128), F32)),
        ],
        [
            pltpu.VMEM((chans, chans), BF16),
            pltpu.VMEM((chans, hidden), BF16),
            pltpu.VMEM((4, chans, tile_cols), F32),
            pltpu.VMEM((2, hidden, 128), F32),
            pltpu.VMEM((RB, hidden, tile_cols), BF16),
        ],
        10 * positions * chans * hidden, 16 * positions * chans,
        (tri, pair_t, d_update, gain, bias, w_gate, o_gain, o_bias, w_out),
    )
    depth_rows = rows // groups
    edge_rows = pl.BlockSpec(
        (groups, depth_rows, 2, tile_rows, tile_cols), lambda s: (0, s, 0, 0, 0)
    )
    (d_chan_edges,) = call(
        d_edges_kernel, "d_edges", (groups,),
        [edge_rows, whole((groups, tokens, tile_cols))],
        [(edge_rows, pltpu.HBM((groups, rows, 2, tile_rows, tile_cols), BF16))],
        [],
        4 * tokens**3, 10 * tokens**2,
        (chan_edges, chan_d_tri.reshape(groups, tokens, tile_cols)),
        in_hbm=(),
    )
    d_edges = exchange(d_chan_edges.reshape(devices, 2, tile_rows, tile_cols))
    (factors,) = call(
        factors_kernel, "factors", (steps,),
        [chanblock, *token_specs, vec, vec, wide],
        [(factorblock, pltpu.HBM((tile_rows, 4 * hidden, tile_cols), BF16))],
        [pltpu.VMEM((4 * hidden, chans), BF16), pltpu.VMEM((2, chans, tile_cols), F32)],
        2 * positions * chans * 4 * hidden, 10 * positions * chans,
        (pair_t, token_mask, token_lanes, gain, bias, w_in),
        in_hbm=(0, 2, 3, 4, 5),
    )
    d_pair, sums = call(
        back_kernel, "back", (steps,),
        [edgeblock, chanblock, chanblock, factorblock, vec, vec, wide, square, square, square,
         whole((hidden, 128))],
        [
            (rowblock, sds((tile_rows, tile_cols, chans), BF16)),
            (whole((chans, 8, 128)), sds((chans, 8, 128), BF16)),
        ],
        [
            pltpu.VMEM((chans, 4 * hidden + chans), BF16),
            pltpu.VMEM((2, chans, tile_cols), F32),
            pltpu.VMEM((2, chans, 128), F32),
            pltpu.VMEM((chans, 4 * hidden), F32),
            pltpu.VMEM((chans * 8, 128), F32),
        ],
        26 * positions * chans * hidden, 16 * positions * chans,
        (d_edges, pair_t, d_gate, factors, gain, bias, w_in, w_gate, sum_gate, sum_out, sum_norm),
        in_hbm=(1, 2, 3, 4, 5, 6, 7),
    )
    part = sds((devices, 8, 128), BF16)
    arrived = exchange(sums)
    (total,) = call(
        functools.partial(total_kernel, 1.0 / tokens), "total", (1,),
        [whole(part.shape)], [(whole(part.shape), part)], [],
        devices * 1024, devices * 8192, (arrived,),
        in_hbm=(),
    )
    everywhere = exchange(total)
    small = [
        (chans, 4 * hidden), (chans, chans), (hidden, chans), (2, chans), (2, hidden),
    ]
    grads = call(
        unpack_kernel, "unpack", (1,),
        [whole((chans, 8, 128))],
        [(whole(shape), sds(shape, F32)) for shape in small],
        [pltpu.VMEM((chans * 8, 128), F32)], 1024, devices * 8192, (everywhere,),
        in_hbm=(),
    )
    return (update, d_pair, *grads)


def solution(mesh):
    return jax.shard_map(
        body,
        mesh=mesh,
        in_specs=(
            P("row", "grp", None),
            P(),
            P(),
            P(),
            P(),
            P(),
            P(),
            P(),
            P(),
            P("row", "grp", None),
        ),
        out_specs=(P("row", "grp", None), P("row", "grp", None), P(), P(), P(), P(), P()),
        check_vma=False,
    )
```
